512 devices in a mesh: seq: 128 (over z, y, x_hi), rep: 4 (over x_lo, core).
Axes of the slice: x: 4 (x_hi: 2, x_lo: 2; x = x_hi * 2 + x_lo), y: 8, z: 8, core: 2. Of those that a mesh axis runs over, the one named last changes fastest.
Arguments:
- queries: bfloat16 [4, 128, 512, 512], P('rep', 'seq'), may hold values from -128 to 128, as said below
- key_vectors: bfloat16 [4, 128, 512, 512], P('rep', 'seq'), may hold values from -6 to 6
- value_vectors: bfloat16 [4, 128, 512, 512], P('rep', 'seq'), may hold values from -6 to 6
- out_grad: bfloat16 [4, 128, 512, 1024], P('rep', 'seq'), may hold values from -6 to 6
- out_weight: bfloat16 [512, 1024], P('seq'), may hold values from -0.25 to 0.25
- row_blocks: int32 [8, 8], replicated, may hold values from 0 to 1, as said below
- column_blocks: int32 [8, 8], replicated, may hold values from 0 to 1, as said below
Outputs:
- query_grad: bfloat16 [4, 128, 512, 512], P('rep', 'seq')
- key_grad: bfloat16 [4, 128, 512, 512], P('rep', 'seq')
- value_grad: bfloat16 [4, 128, 512, 512], P('rep', 'seq')
- weight_grad: float32 [512, 1024], P('seq')
The draws below stay inside these ranges and needn't reach their ends.
Inputs may be any that keep to these rules, and one draw needn't show every extreme that they name: `queries`: query draws may carry large values at some positions. `row_blocks`: entry (i, j) is 1 on the diagonal, 0 above it, 0 or 1 below it. `column_blocks`: entry (i, j) is 1 on the diagonal, 0 above it, 0 or 1 below it.
All inputs are finite; a program needn't handle non-finite values.
Results may differ from the reference program's by a relative error of at most 0.0058.
Values may be sent and summed in bfloat16 or wider, within the bound.
A program may use at most 64 MiB of HBM per device.

```python
import math
import jax
import jax.numpy as jnp
from jax import lax

D = 1024
HEAD_DIM = 128
HEADS_ROW = 2
HEADS_STR = 2
HD = 512
COLS = 512
BLK = 64
ROWS = 128
SBLK = 16
BATCH = 4


def shared_keys(key):
    return jax.random.truncated_normal(key, -6.0, 6.0, (BATCH, ROWS, COLS, HD), jnp.float32)


def draw_key_vectors(key, part):
    base_keys = shared_keys(key)
    return base_keys.astype(jnp.bfloat16)


def draw_queries(key, part):
    key = jax.random.fold_in(key, 2)
    first_key = jax.random.fold_in(key, 0)
    dims_all = (BATCH, ROWS, COLS, HD)
    random_part = jax.random.truncated_normal(first_key, -6.0, 6.0, dims_all, jnp.float32)
    return random_part.astype(jnp.bfloat16)


def block_table(key, number_blocks):
    random_bits = jax.random.randint(key, (number_blocks, number_blocks), 0, 2)
    row_index = jnp.arange(number_blocks)[:, None]
    column_index = jnp.arange(number_blocks)[None, :]
    lower = jnp.where(column_index < row_index, random_bits, 0)
    return jnp.where(column_index == row_index, 1, lower).astype(jnp.int32)


def draw_row_blocks(key, part):
    key = jax.random.fold_in(key, 3)
    return block_table(key, COLS // BLK)


def draw_column_blocks(key, part):
    key = jax.random.fold_in(key, 4)
    return block_table(key, ROWS // SBLK)


def steps_of(stream_key, dims, cuts, low, largest):
    def one(dim, blocks):
        steps = jax.random.uniform(jax.random.fold_in(jax.random.fold_in(stream_key, 6), dim), (blocks,), jnp.float32, low / len(cuts), largest / len(cuts))
        return jnp.repeat(jnp.exp(steps), dims[dim] // blocks).reshape((-1,) + (1,) * (len(dims) - dim - 1))

    gain = one(*cuts[0])
    for cut in cuts[1:]:
        gain = gain * one(*cut)
    return gain


def noise(rng, dims, width, limit, cuts=(), dtype=jnp.bfloat16):
    level = steps_of(rng, dims, cuts, -0.22, 0.18) if cuts else 1.0
    result = jax.random.normal(rng, dims, jnp.float32) * width * level
    return jnp.minimum(jnp.maximum(result, -limit), limit).astype(dtype)


def setup_inputs(seed: int = 0) -> dict:
    splits = jax.random.split(jax.random.key(seed), 8)
    queries = draw_queries(jax.random.fold_in(splits[7], 71), 0)
    key_vectors = draw_key_vectors(jax.random.fold_in(splits[7], 71), 0)
    value_vectors = noise(splits[2], (BATCH, ROWS, COLS, HD), 1.0, 6.0, ((0, 4), (1, 128)))
    out_grad = noise(splits[3], (BATCH, ROWS, COLS, D), 1.0, 6.0, ((0, 4), (1, 128)))
    out_weight = noise(splits[4], (HD, D), HD ** -0.5, 0.25, ((0, 128),))
    row_blocks = draw_row_blocks(jax.random.fold_in(splits[7], 71), 0)
    column_blocks = draw_column_blocks(jax.random.fold_in(splits[7], 71), 0)
    return {"queries": queries, "key_vectors": key_vectors, "value_vectors": value_vectors, "out_grad": out_grad, "out_weight": out_weight, "row_blocks": row_blocks, "column_blocks": column_blocks}


def rounded(values_in):
    return lax.optimization_barrier(values_in.astype(jnp.bfloat16)).astype(jnp.float32)

def allowed_table(blocks, length):
    number_blocks = blocks.shape[0]
    block_width = length // number_blocks
    places = jnp.arange(length) // block_width
    chosen = blocks[places][:, places] == 1
    causal = jnp.arange(length)[None, :] <= jnp.arange(length)[:, None]
    return chosen & causal

def forward_pass(query_in, key_in, value_in, allowed, layout):
    key_layout = layout.replace('q', 'k')
    scores = jnp.einsum(layout + ',' + key_layout + '->nhqk', query_in.astype(jnp.float32), key_in.astype(jnp.float32)) * (1.0 / math.sqrt(HEAD_DIM))
    masked = jnp.where(allowed, scores, -1e+30)
    topmost = lax.optimization_barrier(jnp.max(masked, axis=-1, keepdims=True))
    raised = jnp.exp(masked - topmost)
    attn_probs = raised / lax.optimization_barrier(jnp.sum(raised, axis=-1, keepdims=True))
    prob_round = rounded(attn_probs)
    outputs = jnp.einsum('nhqk,' + key_layout + '->' + layout, prob_round, value_in.astype(jnp.float32)).astype(jnp.bfloat16)
    return (attn_probs, prob_round, outputs)

def backward_pass(attn_probs, prob_round, query_in, key_in, value_in, out_cot, layout):
    key_layout = layout.replace('q', 'k')
    prob_grad = jnp.einsum(layout + ',' + key_layout + '->nhqk', out_cot.astype(jnp.float32), value_in.astype(jnp.float32))
    inner_sum = lax.optimization_barrier(jnp.sum(attn_probs * prob_grad, axis=-1, keepdims=True))
    score_grad = rounded(attn_probs * (prob_grad - inner_sum) * (1.0 / math.sqrt(HEAD_DIM)))
    value_grad = jnp.einsum('nhqk,' + layout + '->' + key_layout, prob_round, out_cot.astype(jnp.float32)).astype(jnp.bfloat16)
    query_grad = jnp.einsum('nhqk,' + key_layout + '->' + layout, score_grad, key_in.astype(jnp.float32)).astype(jnp.bfloat16)
    key_grad = jnp.einsum('nhqk,' + layout + '->' + key_layout, score_grad, query_in.astype(jnp.float32)).astype(jnp.bfloat16)
    return (query_grad, key_grad, value_grad)

def reference(queries, key_vectors, value_vectors, out_grad, out_weight, row_blocks, column_blocks):
    row_width = HEADS_ROW * HEAD_DIM
    flat_grad = out_grad.reshape(BATCH * ROWS * COLS, D)
    attn_grad = jnp.dot(flat_grad, out_weight.T, preferred_element_type=jnp.float32).astype(jnp.bfloat16)
    attn_grad = attn_grad.reshape(BATCH, ROWS, COLS, HD)
    row_allowed = allowed_table(row_blocks, COLS)
    column_allowed = allowed_table(column_blocks, ROWS)

    def row_split(tensor):
        return tensor[..., :row_width].reshape(BATCH * ROWS, 1, COLS, HEADS_ROW, HEAD_DIM)

    def column_split(tensor):
        return tensor[..., row_width:].reshape(BATCH, ROWS, COLS, HEADS_STR, HEAD_DIM)

    def row_work(pieces):
        attn_probs, prob_round, outputs = forward_pass(pieces[0], pieces[1], pieces[2], row_allowed, 'nqhd')
        grads = backward_pass(attn_probs, prob_round, pieces[0], pieces[1], pieces[2], pieces[3], 'nqhd')
        return (outputs,) + grads

    def column_work(pieces):
        attn_probs, prob_round, outputs = forward_pass(pieces[0], pieces[1], pieces[2], column_allowed, 'qnhd')
        grads = backward_pass(attn_probs, prob_round, pieces[0], pieces[1], pieces[2], pieces[3], 'qnhd')
        return (outputs,) + grads
    row_results = lax.map(row_work, (row_split(queries), row_split(key_vectors), row_split(value_vectors), row_split(attn_grad)))
    column_results = lax.map(column_work, (column_split(queries), column_split(key_vectors), column_split(value_vectors), column_split(attn_grad)))
    joined = [jnp.concatenate((row_part.reshape(BATCH, ROWS, COLS, row_width), column_part.reshape(BATCH, ROWS, COLS, HD - row_width)), axis=3) for row_part, column_part in zip(row_results, column_results)]
    attention = joined[0]
    factor = 1.0 / math.sqrt(BATCH * ROWS * COLS)
    weight_grad = jnp.dot(attention.reshape(BATCH * ROWS * COLS, HD).T, flat_grad, preferred_element_type=jnp.float32) * factor
    return (joined[1], joined[2], joined[3], weight_grad)
```

```python
import functools
import math

import jax
import jax.numpy as jnp
from jax import lax
from jax.experimental import pallas as pl
from jax.experimental.pallas import tpu as pltpu
from jax.sharding import PartitionSpec as P

MESH = pl.DeviceIdType.MESH
F32 = jnp.float32
BF16 = jnp.bfloat16
NEG = -1e30

HEAD = 128
SCALE = 1.0 / math.sqrt(HEAD)
COLS = 512
FEAT = 512
MODEL = 1024
SEQ = 128
STEP = 37

W_Z, W_Y, W_X, W_C, G_1, G_2, B_1, B_2, S_C, S_X, S_Y, S_Z, S_R = range(13)


def nn(a, b):
    return lax.dot_general(a, b, (((1,), (0,)), ((), ())), preferred_element_type=F32)


def nt(a, b):
    return lax.dot_general(a, b, (((1,), (1,)), ((), ())), preferred_element_type=F32)


def tn(a, b):
    return lax.dot_general(a, b, (((0,), (0,)), ((), ())), preferred_element_type=F32)


def kernel(
    factor,
    q_hbm, k_hbm, v_hbm, g_hbm, w_hbm, row_tab, col_tab,
    dq_ref, dk_ref, dv_ref, wg_ref,
    q_ref, k_ref, v_ref, g_ref, w_ref,
    w_f32, w_piece, w_z, w_zf, w_qf, w_q, w_x,
    perm, row_bias, col_bias,
    grad, out, probs, dk_acc, dv_acc,
    send1, send2, recv1, recv2, back1, back2, got1, got2,
    stage, stage2, unit_q, unit_k, unit_v, unit_g, unit_p,
    op_t, wg_f, wg_s, wg_c, wg_b, wg_x, wg_cs, wg_y, wg_d, wg_z, wg_e, wg_r,
    in_sem, send_sem, recv_sem,
):
    seq = lax.axis_index("seq")
    rep = lax.axis_index("rep")
    z, y, xh = seq // 16, (seq // 2) % 8, seq % 2
    xl, core = rep // 2, rep % 2

    def place(zz, yy, xx):
        return zz * 16 + yy * 2 + xx

    def turned(step):
        return place((z + step // 16) % 8, (y + (step // 2) % 8) % 8, (xh + step) % 2)

    def remote(src, dst, which, to_seq, to_rep):
        return pltpu.make_async_remote_copy(
            src_ref=src, dst_ref=dst, send_sem=send_sem.at[which], recv_sem=recv_sem.at[which],
            device_id={"seq": to_seq, "rep": to_rep}, device_id_type=MESH,
        )

    def arrived(ref, which):
        pltpu.make_async_copy(ref, ref, recv_sem.at[which]).wait()

    def sent(ref, which):
        pltpu.make_async_copy(ref, ref, send_sem.at[which]).wait()

    loads = [
        pltpu.make_async_copy(a, b, in_sem.at[i])
        for i, (a, b) in enumerate(
            ((w_hbm, w_ref), (q_hbm, q_ref), (k_hbm, k_ref), (v_hbm, v_ref), (g_hbm, g_ref))
        )
    ]
    for load in loads:
        load.start()

    barrier = pltpu.get_barrier_semaphore()

    def greet(to_seq, to_rep):
        pl.semaphore_signal(
            barrier, inc=1, device_id={"seq": to_seq, "rep": to_rep}, device_id_type=MESH
        )

    def greet_step(j, carry):
        greet(turned(j), rep)
        return carry

    lax.fori_loop(1, SEQ, greet_step, 0)
    rep_core = xl * 2 + (1 - core)
    rep_x = (1 - xl) * 2 + core
    rep_both = (1 - xl) * 2 + (1 - core)
    seq_x = place(z, y, 1 - xh)
    greet(seq, rep_core)
    greet(seq, rep_x)
    greet(seq, rep_both)
    greet(seq_x, rep_x)

    loads[0].wait()
    w_val = w_ref[...].astype(F32)
    for b in range(8):
        w_f32[4 * b : 4 * b + 4, :] = w_val[:, 128 * b : 128 * b + 128]
    w_piece[...] = w_f32[...].astype(BF16)
    w_z[pl.ds(z, 1)] = w_piece[...][None]

    def pack(send, first, second):
        for h in range(2):
            lanes = slice(256 + 128 * h, 384 + 128 * h)
            for c in range(4):
                rows = slice(128 * c, 128 * c + 128)
                a = first[rows, lanes].astype(F32).reshape(16, 8, 128)
                b = second[rows, lanes].astype(F32).reshape(16, 8, 128)
                send[64 * h + 16 * c : 64 * h + 16 * c + 16] = jnp.concatenate(
                    (a, b), axis=1
                ).astype(BF16)

    loads[1].wait()
    loads[2].wait()
    pack(send1, q_ref, k_ref)
    recv1[pl.ds(seq, 1)] = send1[pl.ds(seq, 1)]

    def exchange(send, recv, which, low, high):
        def step(j, carry):
            to = turned((j * STEP) % SEQ)
            remote(send.at[to], recv.at[seq], which, to, rep).start()
            return carry

        lax.fori_loop(low, high, step, 0)

    pl.semaphore_wait(barrier, SEQ - 1 + 4)

    for d in (1, 7, 2, 6, 3, 5, 4):
        remote(w_piece, w_z.at[z], W_Z, place((z + d) % 8, y, xh), rep).start()
    exchange(send1, recv1, G_1, 1, 33)

    lane = lax.broadcasted_iota(jnp.int32, (64, 128), 1)
    row = lax.broadcasted_iota(jnp.int32, (64, 128), 0)
    for i in range(8):
        for j in range(i // 2 + 1):
            left = (row_tab[i, 2 * j].astype(F32) - 1.0) * -NEG
            right = (row_tab[i, 2 * j + 1].astype(F32) - 1.0) * -NEG
            bias = jnp.where(lane < 64, left, right)
            if j == i // 2:
                bias = jnp.where(lane + 128 * j <= row + 64 * i, bias, NEG)
            row_bias[64 * i : 64 * i + 64, 128 * j : 128 * j + 128] = bias
    lane = lax.broadcasted_iota(jnp.int32, (16, 128), 1)
    row = lax.broadcasted_iota(jnp.int32, (16, 128), 0)
    for i in range(8):
        bias = jnp.full((16, 128), NEG, F32)
        for j in range(i + 1):
            seen = (col_tab[i, j].astype(F32) - 1.0) * -NEG
            bias = jnp.where(lane // 16 == j, seen, bias)
        col_bias[16 * i : 16 * i + 16, :] = jnp.where(lane <= row + 16 * i, bias, NEG)
    for c in range(8):
        p = lax.broadcasted_iota(jnp.int32, (64, FEAT), 0) + 64 * c
        d = lax.broadcasted_iota(jnp.int32, (64, FEAT), 1)
        natural = ((p >> 2) & 7) * 64 + ((p >> 5) & 7) * 8 + (p >> 8) * 4 + (p & 3)
        perm[64 * c : 64 * c + 64, :] = jnp.where(natural == d, 1.0, 0.0).astype(BF16)

    def row_forward(h):
        lanes = slice(128 * h, 128 * h + 128)
        for b in range(4):
            n = 128 * (b + 1)
            rows = slice(128 * b, n)
            s = nt(q_ref[rows, lanes], k_ref[:n, lanes]) * SCALE + row_bias[rows, :n]
            e = jnp.exp(s - jnp.max(s, axis=1, keepdims=True))
            p = e * (1.0 / jnp.sum(e, axis=1, keepdims=True))
            probs[h, rows, :n] = p
            out[rows, lanes] = nn(p.astype(BF16), v_ref[:n, lanes]).astype(BF16)

    def row_backward(h):
        lanes = slice(128 * h, 128 * h + 128)
        for b in (3, 2, 1, 0):
            n = 128 * (b + 1)
            rows = slice(128 * b, n)
            p = probs[h, rows, :n]
            g = grad[rows, lanes]
            dp = nt(g, v_ref[:n, lanes])
            inner = jnp.sum(p * dp, axis=1, keepdims=True)
            ds = (p * (dp - inner) * SCALE).astype(BF16)
            dq_ref[rows, lanes] = nn(ds, k_ref[:n, lanes]).astype(BF16)
            dv = tn(p.astype(BF16), g)
            dk = tn(ds, q_ref[rows, lanes])
            if b == 3:
                dv_acc[...] = dv
                dk_acc[...] = dk
            else:
                dv_acc[:n, :] += dv
                dk_acc[:n, :] += dk
        dv_ref[:, lanes] = dv_acc[...].astype(BF16)
        dk_ref[:, lanes] = dk_acc[...].astype(BF16)

    arrived(w_z.at[pl.ds(0, 7)], W_Z)
    w_zf[...] = w_z[...].astype(F32).reshape(256, 128)
    for zz in range(8):
        part = w_zf[pl.ds(pl.multiple_of(32 * zz + 8 * rep, 8), 8), :]
        w_qf[4 * zz : 4 * zz + 4, 0:128] = part[0:4]
        w_qf[4 * zz : 4 * zz + 4, 128:256] = part[4:8]
    w_q[...] = w_qf[...].astype(BF16)

    def x_rows(which):
        return pl.ds(pl.multiple_of(which * 256, 256), 256)

    def y_rows(hi, lo):
        return pl.ds(pl.multiple_of(hi * 256 + lo * 32, 32), 32)

    w_x[rep, y_rows(xh, y), :] = w_q[...]
    for d in (1, 7, 2, 6, 3, 5, 4):
        remote(
            w_q, w_x.at[rep, y_rows(xh, y)], W_Y, place(z, (y + d) % 8, xh), rep
        ).start()
    exchange(send1, recv1, G_1, 33, 65)
    loads[3].wait()
    row_forward(0)
    arrived(w_x.at[0, pl.ds(0, 224)], W_Y)
    mine = w_x.at[rep, x_rows(xh)]
    remote(mine, mine, W_X, seq, rep_x).start()
    remote(mine, mine, W_X, seq_x, rep).start()
    remote(mine, mine, W_X, seq_x, rep_x).start()
    exchange(send1, recv1, G_1, 65, 97)
    row_forward(1)
    arrived(w_x.at[pl.ds(0, 3), pl.ds(0, 256)], W_X)
    remote(w_x.at[core], w_x.at[core], W_C, seq, rep_core).start()
    remote(w_x.at[2 + core], w_x.at[2 + core], W_C, seq, rep_core).start()
    exchange(send1, recv1, G_1, 97, SEQ)
    loads[4].wait()
    arrived(w_x.at[pl.ds(0, 2)], W_C)

    for c in range(4):
        rows = slice(128 * c, 128 * c + 128)
        total = nt(g_ref[rows, 0:256], w_x[0])
        for r in range(1, 4):
            total += nt(g_ref[rows, 256 * r : 256 * r + 256], w_x[r])
        grad[rows, :] = nn(total.astype(BF16), perm[...]).astype(BF16)
    pack(send2, v_ref, grad)
    recv2[pl.ds(seq, 1)] = send2[pl.ds(seq, 1)]
    exchange(send2, recv2, G_2, 1, SEQ)

    row_backward(0)
    row_backward(1)

    def spread(recv):
        for c in range(8):
            stage[256 * c : 256 * c + 256, :] = (
                recv[16 * c : 16 * c + 16].astype(F32).reshape(256, 128)
            )

    def gather(send):
        for c in range(8):
            send[16 * c : 16 * c + 16] = (
                stage2[256 * c : 256 * c + 256, :].reshape(16, 16, 128).astype(BF16)
            )

    def unit(u):
        return pl.ds(u, 128, stride=16)

    arrived(recv1.at[pl.ds(0, SEQ - 1)], G_1)
    spread(recv1)
    for u in range(8):
        q = stage[unit(u), :].astype(BF16)
        k = stage[unit(8 + u), :].astype(BF16)
        unit_q[u] = q
        unit_k[u] = k
        s = nt(q, k) * SCALE + col_bias[...]
        e = jnp.exp(s - jnp.max(s, axis=1, keepdims=True))
        unit_p[u] = e * (1.0 / jnp.sum(e, axis=1, keepdims=True))

    arrived(recv2.at[pl.ds(0, SEQ - 1)], G_2)
    spread(recv2)
    for u in range(8):
        v = stage[unit(u), :].astype(BF16)
        g = stage[unit(8 + u), :].astype(BF16)
        unit_v[u] = v
        unit_g[u] = g
        p = unit_p[u].astype(BF16)
        stage2[unit(u), :] = nn(p, v)
        stage2[unit(8 + u), :] = tn(p, g)
    gather(back1)
    got1[pl.ds(seq, 1)] = back1[pl.ds(seq, 1)]
    exchange(back1, got1, B_1, 1, SEQ)
    for u in range(8):
        p = unit_p[u]
        dp = nt(unit_g[u], unit_v[u])
        inner = jnp.sum(p * dp, axis=1, keepdims=True)
        ds = (p * (dp - inner) * SCALE).astype(BF16)
        stage2[unit(u), :] = nn(ds, unit_k[u])
        stage2[unit(8 + u), :] = tn(ds, unit_q[u])
    gather(back2)
    got2[pl.ds(seq, 1)] = back2[pl.ds(seq, 1)]
    exchange(back2, got2, B_2, 1, SEQ)

    def unpack(got, first, second):
        for h in range(2):
            lanes = slice(256 + 128 * h, 384 + 128 * h)
            for c in range(4):
                rows = slice(128 * c, 128 * c + 128)
                both = got[64 * h + 16 * c : 64 * h + 16 * c + 16].astype(F32)
                first[rows, lanes] = both[:, 0:8, :].reshape(128, 128).astype(BF16)
                second[rows, lanes] = both[:, 8:16, :].reshape(128, 128).astype(BF16)

    arrived(got1.at[pl.ds(0, SEQ - 1)], B_1)
    unpack(got1, out, dv_ref)

    for c in range(4):
        rows = slice(128 * c, 128 * c + 128)
        op_t[rows, :] = nt(perm[rows, :], out[...]).astype(BF16)
    for c in range(4):
        rows = slice(128 * c, 128 * c + 128)
        for r in range(4):
            term = nn(op_t[rows, :], g_ref[:, 256 * r : 256 * r + 256])
            wg_f[r, rows, :] = term
            wg_s[r, rows, :] = term.astype(BF16)
    remote(wg_s.at[1 - core], wg_c.at[0], S_C, seq, rep_core).start()
    remote(wg_s.at[3 - core], wg_c.at[1], S_C, seq, rep_core).start()
    arrived(wg_c, S_C)
    for i in range(2):
        for c in range(4):
            rows = slice(128 * c, 128 * c + 128)
            wg_b[i, rows, :] = (
                wg_f[2 * i + core, rows, :] + wg_c[i, rows, :].astype(F32)
            ).astype(BF16)
    here = xh * 2 + xl
    remote(wg_b.at[1 - xl, x_rows(xh)], wg_x.at[here], S_X, seq, rep_x).start()
    remote(wg_b.at[xl, x_rows(1 - xh)], wg_x.at[here], S_X, seq_x, rep).start()
    remote(wg_b.at[1 - xl, x_rows(1 - xh)], wg_x.at[here], S_X, seq_x, rep_x).start()
    wg_x[pl.ds(here, 1)] = wg_b[pl.ds(xl, 1), x_rows(xh), :]
    arrived(wg_x.at[pl.ds(0, 3)], S_X)
    total = wg_x[0].astype(F32)
    for i in range(1, 4):
        total += wg_x[i].astype(F32)
    wg_cs[...] = total.astype(BF16)
    for d in (1, 7, 2, 6, 3, 5, 4):
        to = (y + d) % 8
        remote(
            wg_cs.at[pl.ds(pl.multiple_of(to * 32, 32), 32)], wg_y.at[y], S_Y,
            place(z, to, xh), rep,
        ).start()
    wg_y[pl.ds(y, 1)] = wg_cs[pl.ds(pl.multiple_of(y * 32, 32), 32), :][None]
    arrived(wg_y.at[pl.ds(0, 7)], S_Y)
    total = wg_y[0].astype(F32)
    for i in range(1, 8):
        total += wg_y[i].astype(F32)
    wg_d[...] = total
    for d in (1, 7, 2, 6, 3, 5, 4):
        to = (z + d) % 8
        remote(
            wg_d.at[pl.ds(pl.multiple_of(to // 2 * 8, 8), 8)], wg_z.at[z], S_Z,
            place(to, y, xh), rep,
        ).start()
    wg_z[pl.ds(z, 1)] = wg_d[pl.ds(pl.multiple_of(z // 2 * 8, 8), 8), :][None]
    arrived(wg_z.at[pl.ds(0, 7)], S_Z)
    total = wg_z[0]
    for i in range(1, 8):
        total += wg_z[i]
    wg_e[...] = total * factor
    for to in (rep_core, rep_x, rep_both):
        remote(wg_e, wg_r.at[rep], S_R, seq, to).start()
    wg_r[pl.ds(rep, 1)] = wg_e[...][None]
    arrived(wg_r.at[pl.ds(0, 3)], S_R)
    odd = (z % 2) == 1
    for r in range(4):
        both = wg_r[r]
        wg_ref[:, 256 * r : 256 * r + 256] = jnp.where(odd, both[4:8, :], both[0:4, :])

    arrived(got2.at[pl.ds(0, SEQ - 1)], B_2)
    unpack(got2, dq_ref, dk_ref)

    sent(w_z.at[pl.ds(0, 7)], W_Z)
    sent(w_x.at[0, pl.ds(0, 224)], W_Y)
    sent(w_x.at[pl.ds(0, 3), pl.ds(0, 256)], W_X)
    sent(w_x.at[pl.ds(0, 2)], W_C)
    for which, ref in ((G_1, send1), (G_2, send2), (B_1, back1), (B_2, back2)):
        sent(ref.at[pl.ds(0, SEQ - 1)], which)
    sent(wg_c, S_C)
    sent(wg_x.at[pl.ds(0, 3)], S_X)
    sent(wg_y.at[pl.ds(0, 7)], S_Y)
    sent(wg_z.at[pl.ds(0, 7)], S_Z)
    sent(wg_r.at[pl.ds(0, 3)], S_R)


def body(queries, key_vectors, value_vectors, out_grad, out_weight, row_blocks, column_blocks):
    token_count = lax.axis_size("rep") * lax.axis_size("seq") * COLS
    factor = 1.0 / math.sqrt(token_count)
    vmem = pltpu.VMEM
    hbm = pl.BlockSpec(memory_space=pl.ANY)
    smem = pl.BlockSpec(memory_space=pltpu.SMEM)
    whole = pl.BlockSpec(memory_space=pltpu.VMEM)
    grads = jax.ShapeDtypeStruct((COLS, FEAT), BF16)
    pieces = vmem((SEQ, 16, 128), BF16)
    units = vmem((8, 128, 128), BF16)
    scratch = [
        vmem((COLS, FEAT), BF16), vmem((COLS, FEAT), BF16), vmem((COLS, FEAT), BF16),
        vmem((COLS, MODEL), BF16), vmem((4, MODEL), BF16),
        vmem((32, 128), F32), vmem((32, 128), BF16), vmem((8, 32, 128), BF16),
        vmem((256, 128), F32), vmem((32, 256), F32), vmem((32, 256), BF16),
        vmem((4, FEAT, 256), BF16),
        vmem((FEAT, FEAT), BF16), vmem((COLS, COLS), F32), vmem((SEQ, SEQ), F32),
        vmem((COLS, FEAT), BF16), vmem((COLS, FEAT), BF16), vmem((2, COLS, COLS), F32),
        vmem((COLS, HEAD), F32), vmem((COLS, HEAD), F32),
        pieces, pieces, pieces, pieces, pieces, pieces, pieces, pieces,
        vmem((SEQ * 16, 128), F32), vmem((SEQ * 16, 128), F32),
        units, units, units, units, vmem((8, 128, 128), F32),
        vmem((FEAT, COLS), BF16), vmem((4, FEAT, 256), F32), vmem((4, FEAT, 256), BF16),
        vmem((2, FEAT, 256), BF16), vmem((2, FEAT, 256), BF16), vmem((4, 256, 256), BF16),
        vmem((256, 256), BF16), vmem((8, 32, 256), BF16), vmem((32, 256), F32),
        vmem((8, 8, 256), F32), vmem((8, 256), F32), vmem((4, 8, 256), F32),
        pltpu.SemaphoreType.DMA((5,)),
        pltpu.SemaphoreType.DMA((13,)),
        pltpu.SemaphoreType.DMA((13,)),
    ]
    query_grad, key_grad, value_grad, weight_grad = pl.pallas_call(
        functools.partial(kernel, factor),
        out_shape=(grads, grads, grads, jax.ShapeDtypeStruct((4, MODEL), F32)),
        in_specs=[hbm] * 5 + [smem] * 2,
        out_specs=(whole, whole, whole, whole),
        scratch_shapes=scratch,
        compiler_params=pltpu.CompilerParams(
            collective_id=0, has_side_effects=True, vmem_limit_bytes=56 * 2**20
        ),
        cost_estimate=pl.CostEstimate(
            flops=2_500_000_000, bytes_accessed=5_000_000, transcendentals=800_000
        ),
    )(
        queries.reshape(COLS, FEAT), key_vectors.reshape(COLS, FEAT),
        value_vectors.reshape(COLS, FEAT), out_grad.reshape(COLS, MODEL),
        out_weight, row_blocks, column_blocks,
    )
    shape = (1, 1, COLS, FEAT)
    return (
        query_grad.reshape(shape), key_grad.reshape(shape), value_grad.reshape(shape), weight_grad
    )


def solution(mesh):
    return jax.shard_map(
        body,
        mesh=mesh,
        in_specs=(
            P("rep", "seq", None, None),
            P("rep", "seq", None, None),
            P("rep", "seq", None, None),
            P("rep", "seq", None, None),
            P("seq", None),
            P(),
            P(),
        ),
        out_specs=(
            P("rep", "seq", None, None),
            P("rep", "seq", None, None),
            P("rep", "seq", None, None),
            P("seq", None),
        ),
        check_vma=False,
    )
```

```python
import functools
import math

import jax
import jax.numpy as jnp
from jax import lax
from jax.experimental import pallas as pl
from jax.experimental.pallas import tpu as pltpu
from jax.sharding import PartitionSpec as P

MESH = pl.DeviceIdType.MESH
F32 = jnp.float32
BF16 = jnp.bfloat16
NEG = -1e30

HEAD = 128
SCALE = 1.0 / math.sqrt(HEAD)
COLS = 512
FEAT = 512
MODEL = 1024
SEQ = 128

(
    W_ROW, W_STR, X_ROW, X_STR, C_ROW, C_STR, G_QK, G_V, G_G, B_O, B_V, B_QK,
    TC_ROW, TC_STR, TX_ROW, TX_STR, S_ALL, S_REP,
) = range(18)


def nn(a, b):
    return lax.dot_general(a, b, (((1,), (0,)), ((), ())), preferred_element_type=F32)


def nt(a, b):
    return lax.dot_general(a, b, (((1,), (1,)), ((), ())), preferred_element_type=F32)


def tn(a, b):
    return lax.dot_general(a, b, (((0,), (0,)), ((), ())), preferred_element_type=F32)


def kernel(
    factor,
    q_hbm, k_hbm, v_hbm, g_hbm, w_hbm, row_hbm, col_hbm,
    dq_ref, dk_ref, dv_ref, wg_ref,
    q_ref, k_ref, v_ref, g_ref, w_ref, row_tab, col_tab,
    w_f32, w_own, w_got, w_x, row_bias, col_bias,
    grad, out, probs, dk_acc, dv_acc,
    send_qk, send_v, send_g, recv_qk, recv_v, recv_g,
    back_o, back_v, back_qk, got_o, got_v, got_qk,
    stage, stage2, unit_q, unit_k, unit_v, unit_g, unit_p,
    term, term_b, term_got, term_own, term_away, term_near, sum_own, sum_got, last_own, last_got,
    in_sem, send_sem, recv_sem,
):
    seq = lax.axis_index("seq")
    rep = lax.axis_index("rep")
    z, y, xh = seq // 16, (seq // 2) % 8, seq % 2
    xl, core = rep // 2, rep % 2

    def remote(src, dst, which, to_seq, to_rep):
        return pltpu.make_async_remote_copy(
            src_ref=src, dst_ref=dst, send_sem=send_sem.at[which], recv_sem=recv_sem.at[which],
            device_id={"seq": to_seq, "rep": to_rep}, device_id_type=MESH,
        )

    def arrived(ref, which):
        pltpu.make_async_copy(ref, ref, recv_sem.at[which]).wait()

    def sent(ref, which):
        pltpu.make_async_copy(ref, ref, send_sem.at[which]).wait()

    loads = [
        pltpu.make_async_copy(a, b, in_sem.at[i])
        for i, (a, b) in enumerate(
            (
                (w_hbm, w_ref), (q_hbm, q_ref), (k_hbm, k_ref), (v_hbm, v_ref), (g_hbm, g_ref),
                (row_hbm, row_tab), (col_hbm, col_tab),
            )
        )
    ]
    for load in loads:
        load.start()

    around = [(d, x) for d in (4, 3, 5, 2, 6, 1, 7, 0) for x in (1, 0)]
    sides = [(((y + d) % 8) * 2 + (xh + x) % 2, 3 * (2 * d + x) + 1) for d, x in around]

    def rounds(one, low, high):
        def step(turn, carry):
            for i in range(16):
                one(((z + turn + sides[i][1]) % 8) * 16 + sides[i][0])
            return carry

        lax.fori_loop(low, min(high, 7), step, 0)
        if high == 8:
            for i in range(16):
                distance = (7 + sides[i][1]) % 8
                if around[i] != (0, 0) or distance != 0:
                    one(((z + distance) % 8) * 16 + sides[i][0])

    barrier = pltpu.get_barrier_semaphore()

    def greet(to_seq, to_rep):
        pl.semaphore_signal(
            barrier, inc=1, device_id={"seq": to_seq, "rep": to_rep}, device_id_type=MESH
        )

    rounds(lambda to: greet(to, rep), 0, 8)
    rep_core, rep_x = xl * 2 + (1 - core), (1 - xl) * 2 + core
    others = [rep_core, rep_x, (1 - xl) * 2 + (1 - core)]
    for to in others:
        greet(seq, to)

    loads[0].wait()
    w_val = w_ref[...].astype(F32)
    for b in range(8):
        w_f32[4 * b : 4 * b + 4, :] = w_val[:, 128 * b : 128 * b + 128]
    w_own[...] = w_f32[pl.ds(pl.multiple_of(8 * rep, 8), 8), :].astype(BF16)
    w_got[pl.ds(seq, 1)] = w_own[...][None]

    def pack(send, *tensors):
        for h in range(2):
            lanes = slice(256 + 128 * h, 384 + 128 * h)
            for c in range(4):
                rows = slice(128 * c, 128 * c + 128)
                parts = [t[rows, lanes].astype(F32).reshape(16, 8, 128) for t in tensors]
                whole = parts[0] if len(parts) == 1 else jnp.concatenate(parts, axis=1)
                send[64 * h + 16 * c : 64 * h + 16 * c + 16] = whole.astype(BF16)

    def keep(send, recv):
        recv[pl.ds(seq, 1)] = send[pl.ds(seq, 1)]

    loads[1].wait()
    loads[2].wait()
    pack(send_qk, q_ref, k_ref)
    keep(send_qk, recv_qk)
    loads[3].wait()
    pack(send_v, v_ref)
    keep(send_v, recv_v)

    def exchange(send, recv, which, low, high):
        def one(to):
            remote(send.at[to], recv.at[seq], which, to, rep).start()

        rounds(one, low, high)

    def share_weights(which):
        def one(to):
            remote(w_own, w_got.at[seq], which, to, rep).start()

        rounds(one, 0, 8)

    pl.semaphore_wait(barrier, SEQ - 1 + 3)

    def spread(recv, count):
        for c in range(8):
            stage[16 * count * c : 16 * count * (c + 1), :] = (
                recv[16 * c : 16 * c + 16].astype(F32).reshape(16 * count, 128)
            )

    def gather(send, count):
        for c in range(8):
            send[16 * c : 16 * c + 16] = (
                stage2[16 * count * c : 16 * count * (c + 1), :]
                .reshape(16, count, 128)
                .astype(BF16)
            )

    def unit(u, count):
        return pl.ds(u, 128, stride=count)

    def whole(ref):
        return ref.at[pl.ds(0, SEQ - 1)]

    strided = z >= 4

    @pl.when(strided)
    def _():
        share_weights(W_STR)

    exchange(send_qk, recv_qk, G_QK, 0, 8)

    loads[5].wait()
    loads[6].wait()
    lane = lax.broadcasted_iota(jnp.int32, (64, 128), 1)
    row = lax.broadcasted_iota(jnp.int32, (64, 128), 0)
    for i in range(8):
        for j in range(i // 2 + 1):
            left = (row_tab[i, 2 * j].astype(F32) - 1.0) * -NEG
            right = (row_tab[i, 2 * j + 1].astype(F32) - 1.0) * -NEG
            bias = jnp.where(lane < 64, left, right)
            if j == i // 2:
                bias = jnp.where(lane + 128 * j <= row + 64 * i, bias, NEG)
            row_bias[64 * i : 64 * i + 64, 128 * j : 128 * j + 128] = bias
    lane = lax.broadcasted_iota(jnp.int32, (16, 128), 1)
    row = lax.broadcasted_iota(jnp.int32, (16, 128), 0)
    for i in range(8):
        bias = jnp.full((16, 128), NEG, F32)
        for j in range(i + 1):
            seen = (col_tab[i, j].astype(F32) - 1.0) * -NEG
            bias = jnp.where(lane // 16 == j, seen, bias)
        col_bias[16 * i : 16 * i + 16, :] = jnp.where(lane <= row + 16 * i, bias, NEG)
    def row_forward(h):
        lanes = slice(128 * h, 128 * h + 128)
        for b in range(4):
            n = 128 * (b + 1)
            rows = slice(128 * b, n)
            s = nt(q_ref[rows, lanes], k_ref[:n, lanes]) * SCALE + row_bias[rows, :n]
            e = jnp.exp(s - jnp.max(s, axis=1, keepdims=True))
            p = e * (1.0 / jnp.sum(e, axis=1, keepdims=True))
            probs[h, rows, :n] = p
            out[rows, lanes] = nn(p.astype(BF16), v_ref[:n, lanes]).astype(BF16)

    def row_backward(h):
        lanes = slice(128 * h, 128 * h + 128)
        for b in (3, 2, 1, 0):
            n = 128 * (b + 1)
            rows = slice(128 * b, n)
            p = probs[h, rows, :n]
            g = grad[rows, lanes]
            dp = nt(g, v_ref[:n, lanes])
            inner = jnp.sum(p * dp, axis=1, keepdims=True)
            ds = (p * (dp - inner) * SCALE).astype(BF16)
            dq_ref[rows, lanes] = nn(ds, k_ref[:n, lanes]).astype(BF16)
            dv = tn(p.astype(BF16), g)
            dk = tn(ds, q_ref[rows, lanes])
            if b == 3:
                dv_acc[...] = dv
                dk_acc[...] = dk
            else:
                dv_acc[:n, :] += dv
                dk_acc[:n, :] += dk
        dv_ref[:, lanes] = dv_acc[...].astype(BF16)
        dk_ref[:, lanes] = dk_acc[...].astype(BF16)

    upper = lax.broadcasted_iota(jnp.int32, (32, 8, 128), 1) < 4

    def arrived_weights(which, mine, half):
        @pl.when(mine)
        def _():
            arrived(w_got.at[pl.ds(0, 63)], which)

        @pl.when(jnp.logical_not(mine))
        def _():
            arrived(w_got.at[pl.ds(0, 64)], which)

        pairs = w_got[64 * half : 64 * half + 64].astype(F32).reshape(32, 2, 8, 128)
        even, odd = pairs[:, 0], pairs[:, 1]
        left = jnp.where(upper, even, pltpu.roll(odd, 4, 1)).reshape(256, 128)
        right = jnp.where(upper, pltpu.roll(even, 4, 1), odd).reshape(256, 128)
        w_x[pl.ds(half, 1), pl.ds(rep, 1)] = (
            jnp.concatenate((left, right), axis=1).astype(BF16)[None, None]
        )

    def share_quarter(which_x, which_core, half):
        mine = w_x.at[half, rep]
        remote(mine, mine, which_x, seq, rep_x).start()
        remote(mine, mine, which_core, seq, rep_core).start()

    def relay_quarter(which_x, which_core, half):
        arrived(w_x.at[half, 0], which_x)
        theirs = w_x.at[half, rep_x]
        remote(theirs, theirs, which_core, seq, rep_core).start()

    def arrived_quarters(which_core, half):
        arrived(w_x.at[half, pl.ds(0, 2)], which_core)

    def quarters(ref):
        return ref.at[pl.ds(0, 3)]

    def attention_gradient(half):
        for c in range(4):
            rows = slice(128 * c, 128 * c + 128)
            total = nt(g_ref[rows, 0:256], w_x[half, 0])
            for r in range(1, 4):
                total += nt(g_ref[rows, 256 * r : 256 * r + 256], w_x[half, r])
            grad[rows, 256 * half : 256 * half + 256] = total.astype(BF16)

    def weight_terms(half, which):
        lanes = slice(256 * half, 256 * half + 256)
        for r in range(4):
            product = tn(out[:, lanes], g_ref[:, 256 * r : 256 * r + 256])
            term[half, r] = product
            term_b[half, r] = product.astype(BF16)
        for i in range(2):
            remote(
                term_b.at[half, 2 * i + 1 - core], term_got.at[half, i], which, seq, rep_core
            ).start()

    def chip_sums(half, which_core, which_x):
        arrived(term_got.at[half], which_core)
        term_own[half] = term[half, rep] + term_got[half, xl].astype(F32)
        term_away[half] = (term[half, rep_x] + term_got[half, 1 - xl].astype(F32)).astype(BF16)
        remote(term_away.at[half], term_near.at[half], which_x, seq, rep_x).start()

    def weight_sums(half, which_x):
        arrived(term_near.at[half], which_x)
        total = term_own[half] + term_near[half].astype(F32)
        left = total[:, 0:128].reshape(32, 8, 128)
        right = total[:, 128:256].reshape(32, 8, 128)
        even = jnp.where(upper, left, pltpu.roll(right, 4, 1))
        odd = jnp.where(upper, pltpu.roll(left, 4, 1), right)
        sum_own[64 * half : 64 * half + 64] = (
            jnp.stack((even, odd), axis=1).reshape(64, 8, 128).astype(BF16)
        )

        def one(to):
            remote(sum_own.at[to], sum_got.at[seq], S_ALL, to, rep).start()

        def step(turn, carry):
            for i in range(16):
                if around[i] != (0, 0):
                    one((4 * half + (z + turn + sides[i][1]) % 4) * 16 + sides[i][0])
            return carry

        lax.fori_loop(0, 4, step, 0)
        here = sides[-1][0]
        for d in (1, 2, 3):
            one((4 * half + (z + d) % 4) * 16 + here)
        mine = z // 4 == half

        @pl.when(jnp.logical_not(mine))
        def _():
            one((4 * half + z % 4) * 16 + here)

        @pl.when(mine)
        def _():
            sum_got[pl.ds(seq, 1)] = sum_own[pl.ds(seq, 1)]

    row_forward(0)
    row_forward(1)
    arrived_weights(W_STR, strided, 1)
    share_quarter(X_STR, C_STR, 1)
    exchange(send_v, recv_v, G_V, 0, 8)

    @pl.when(jnp.logical_not(strided))
    def _():
        share_weights(W_ROW)

    loads[4].wait()
    weight_terms(0, TC_ROW)
    relay_quarter(X_STR, C_STR, 1)
    chip_sums(0, TC_ROW, TX_ROW)
    arrived_quarters(C_STR, 1)
    attention_gradient(1)
    pack(send_g, grad)
    keep(send_g, recv_g)
    exchange(send_g, recv_g, G_G, 0, 8)

    arrived(whole(recv_qk), G_QK)
    spread(recv_qk, 16)
    for u in range(8):
        q = stage[unit(u, 16), :].astype(BF16)
        k = stage[unit(8 + u, 16), :].astype(BF16)
        unit_q[u] = q
        unit_k[u] = k
        s = nt(q, k) * SCALE + col_bias[...]
        e = jnp.exp(s - jnp.max(s, axis=1, keepdims=True))
        unit_p[u] = e * (1.0 / jnp.sum(e, axis=1, keepdims=True))
    arrived(whole(recv_v), G_V)
    spread(recv_v, 8)
    for u in range(8):
        v = stage[unit(u, 8), :].astype(BF16)
        unit_v[u] = v
        stage2[unit(u, 8), :] = nn(unit_p[u].astype(BF16), v)
    gather(back_o, 8)
    keep(back_o, got_o)
    sent(whole(send_qk), G_QK)
    sent(whole(send_v), G_V)
    exchange(back_o, got_o, B_O, 0, 8)

    arrived_weights(W_ROW, jnp.logical_not(strided), 0)
    share_quarter(X_ROW, C_ROW, 0)
    arrived(whole(recv_g), G_G)
    spread(recv_g, 8)
    for u in range(8):
        g = stage[unit(u, 8), :].astype(BF16)
        unit_g[u] = g
        stage2[unit(u, 8), :] = tn(unit_p[u].astype(BF16), g)
    gather(back_v, 8)
    keep(back_v, got_v)
    sent(whole(send_g), G_G)
    sent(whole(back_o), B_O)
    exchange(back_v, got_v, B_V, 0, 8)
    for u in range(8):
        p = unit_p[u]
        dp = nt(unit_g[u], unit_v[u])
        inner = jnp.sum(p * dp, axis=1, keepdims=True)
        ds = (p * (dp - inner) * SCALE).astype(BF16)
        stage2[unit(u, 16), :] = nn(ds, unit_k[u])
        stage2[unit(8 + u, 16), :] = tn(ds, unit_q[u])
    gather(back_qk, 16)
    keep(back_qk, got_qk)
    exchange(back_qk, got_qk, B_QK, 0, 8)

    def unpack(got, *tensors):
        for h in range(2):
            lanes = slice(256 + 128 * h, 384 + 128 * h)
            for c in range(4):
                rows = slice(128 * c, 128 * c + 128)
                part = got[64 * h + 16 * c : 64 * h + 16 * c + 16].astype(F32)
                for i, t in enumerate(tensors):
                    t[rows, lanes] = part[:, 8 * i : 8 * i + 8, :].reshape(128, 128).astype(BF16)

    relay_quarter(X_ROW, C_ROW, 0)
    weight_sums(0, TX_ROW)
    arrived(whole(got_o), B_O)
    unpack(got_o, out)
    weight_terms(1, TC_STR)
    arrived_quarters(C_ROW, 0)
    attention_gradient(0)
    chip_sums(1, TC_STR, TX_STR)
    row_backward(0)
    row_backward(1)
    weight_sums(1, TX_STR)

    arrived(whole(sum_got), S_ALL)
    total = sum_got[0:16].astype(F32)
    for i in range(1, 8):
        total += sum_got[16 * i : 16 * i + 16].astype(F32)
    total = jnp.sum(total, axis=0)
    last_own[...] = total * factor
    for to in others:
        remote(last_own, last_got.at[rep], S_REP, seq, to).start()
    last_got[pl.ds(rep, 1)] = last_own[...][None]
    arrived(quarters(last_got), S_REP)
    for r in range(4):
        wg_ref[:, 256 * r : 256 * r + 128] = last_got[r, 0:4, :]
        wg_ref[:, 256 * r + 128 : 256 * r + 256] = last_got[r, 4:8, :]

    arrived(whole(got_v), B_V)
    unpack(got_v, dv_ref)
    arrived(whole(got_qk), B_QK)
    unpack(got_qk, dq_ref, dk_ref)

    @pl.when(strided)
    def _():
        sent(whole(w_got), W_STR)

    @pl.when(jnp.logical_not(strided))
    def _():
        sent(whole(w_got), W_ROW)

    for half, which_x, which_core in ((0, X_ROW, C_ROW), (1, X_STR, C_STR)):
        sent(w_x.at[half, 0], which_x)
        sent(w_x.at[half, pl.ds(0, 2)], which_core)
    for which, ref in ((B_V, back_v), (B_QK, back_qk),):
        sent(whole(ref), which)
    for half, which_core, which_x in ((0, TC_ROW, TX_ROW), (1, TC_STR, TX_STR)):
        sent(term_got.at[half], which_core)
        sent(term_near.at[half], which_x)
    sent(whole(sum_got), S_ALL)
    sent(quarters(last_got), S_REP)


def finish(*refs):
    for i in range(4):
        refs[4 + i][...] = refs[i][...]


def body(queries, key_vectors, value_vectors, out_grad, out_weight, row_blocks, column_blocks):
    token_count = lax.axis_size("rep") * lax.axis_size("seq") * COLS
    factor = 1.0 / math.sqrt(token_count)
    vmem = pltpu.VMEM
    hbm = pl.BlockSpec(memory_space=pl.ANY)
    whole = pl.BlockSpec(memory_space=pltpu.VMEM)
    grads = jax.ShapeDtypeStruct((COLS, FEAT), BF16)
    one = vmem((SEQ, 8, 128), BF16)
    two = vmem((SEQ, 16, 128), BF16)
    units = vmem((8, 128, 128), BF16)
    scratch = [
        vmem((COLS, FEAT), BF16), vmem((COLS, FEAT), BF16), vmem((COLS, FEAT), BF16),
        vmem((COLS, MODEL), BF16), vmem((4, MODEL), BF16),
        pltpu.SMEM((8, 8), jnp.int32), pltpu.SMEM((8, 8), jnp.int32),
        vmem((32, 128), F32), vmem((8, 128), BF16), one, vmem((2, 4, 256, 256), BF16),
        vmem((COLS, COLS), F32), vmem((SEQ, SEQ), F32),
        vmem((COLS, FEAT), BF16), vmem((COLS, FEAT), BF16), vmem((2, COLS, COLS), F32),
        vmem((COLS, HEAD), F32), vmem((COLS, HEAD), F32),
        two, one, one, two, one, one, one, one, two, one, one, two,
        vmem((SEQ * 16, 128), F32), vmem((SEQ * 16, 128), F32),
        units, units, units, units, vmem((8, 128, 128), F32),
        vmem((2, 4, 256, 256), F32), vmem((2, 4, 256, 256), BF16), vmem((2, 2, 256, 256), BF16),
        vmem((2, 256, 256), F32), vmem((2, 256, 256), BF16), vmem((2, 256, 256), BF16),
        one, one, vmem((8, 128), F32), vmem((4, 8, 128), F32),
        pltpu.SemaphoreType.DMA((7,)),
        pltpu.SemaphoreType.DMA((18,)),
        pltpu.SemaphoreType.DMA((18,)),
    ]
    results = (grads, grads, grads, jax.ShapeDtypeStruct((4, MODEL), F32))
    raw = pl.pallas_call(
        functools.partial(kernel, factor),
        out_shape=results,
        in_specs=[hbm] * 7,
        out_specs=(whole, whole, whole, whole),
        scratch_shapes=scratch,
        compiler_params=pltpu.CompilerParams(
            collective_id=0, has_side_effects=True, vmem_limit_bytes=56 * 2**20
        ),
        cost_estimate=pl.CostEstimate(
            flops=2_500_000_000, bytes_accessed=5_000_000, transcendentals=800_000
        ),
    )(
        queries.reshape(COLS, FEAT), key_vectors.reshape(COLS, FEAT),
        value_vectors.reshape(COLS, FEAT), out_grad.reshape(COLS, MODEL),
        out_weight, row_blocks, column_blocks,
    )
    query_grad, key_grad, value_grad, weight_grad = pl.pallas_call(
        finish,
        out_shape=results,
        in_specs=[whole] * 4,
        out_specs=(whole,) * 4,
    )(*raw)
    shape = (1, 1, COLS, FEAT)
    return (
        query_grad.reshape(shape), key_grad.reshape(shape), value_grad.reshape(shape), weight_grad
    )


def solution(mesh):
    return jax.shard_map(
        body,
        mesh=mesh,
        in_specs=(
            P("rep", "seq", None, None),
            P("rep", "seq", None, None),
            P("rep", "seq", None, None),
            P("rep", "seq", None, None),
            P("seq", None),
            P(),
            P(),
        ),
        out_specs=(
            P("rep", "seq", None, None),
            P("rep", "seq", None, None),
            P("rep", "seq", None, None),
            P("seq", None),
        ),
        check_vma=False,
    )
```

```python
import functools
import math

import jax
import jax.numpy as jnp
from jax import lax
from jax.experimental import pallas as pl
from jax.experimental.pallas import tpu as pltpu
from jax.sharding import PartitionSpec as P

MESH = pl.DeviceIdType.MESH
F32 = jnp.float32
BF16 = jnp.bfloat16
NEG = -1e30

HEAD = 128
SCALE = 1.0 / math.sqrt(HEAD)
COLS = 512
FEAT = 512
MODEL = 1024
SEQ = 128

(
    W_ROW, W_STR, X_ROW, X_STR, C_ROW, C_STR, G_QK, G_V, G_G, B_O, B_V, B_QK,
    TC_ROW, TC_STR, TX_ROW, TX_STR, S_ALL, S_REP,
) = range(18)


def nn(a, b):
    return lax.dot_general(a, b, (((1,), (0,)), ((), ())), preferred_element_type=F32)


def nt(a, b):
    return lax.dot_general(a, b, (((1,), (1,)), ((), ())), preferred_element_type=F32)


def tn(a, b):
    return lax.dot_general(a, b, (((0,), (0,)), ((), ())), preferred_element_type=F32)


def kernel(
    factor,
    q_hbm, k_hbm, v_hbm, g_hbm, w_hbm, row_hbm, col_hbm,
    dq_hbm, dk_hbm, dv_hbm, wg_hbm,
    dq_ref, dk_ref, dv_ref, wg_ref,
    q_ref, k_ref, v_ref, g_ref, w_ref, row_tab, col_tab,
    w_f32, w_own, w_got, w_x, row_bias, col_bias,
    grad, out, probs, dk_acc, dv_acc,
    send_qk, send_v, send_g, recv_qk, recv_v, recv_g,
    back_o, back_v, back_qk, got_o, got_v, got_qk,
    stage, stage2, unit_q, unit_k, unit_v, unit_g, unit_p,
    term, term_b, term_got, term_own, term_away, term_near, sum_own, sum_got, last_own, last_got,
    in_sem, out_sem, send_sem, recv_sem,
):
    seq = lax.axis_index("seq")
    rep = lax.axis_index("rep")
    z, y, xh = seq // 16, (seq // 2) % 8, seq % 2
    xl, core = rep // 2, rep % 2

    def remote(src, dst, which, to_seq, to_rep):
        return pltpu.make_async_remote_copy(
            src_ref=src, dst_ref=dst, send_sem=send_sem.at[which], recv_sem=recv_sem.at[which],
            device_id={"seq": to_seq, "rep": to_rep}, device_id_type=MESH,
        )

    def arrived(ref, which):
        pltpu.make_async_copy(ref, ref, recv_sem.at[which]).wait()

    def sent(ref, which):
        pltpu.make_async_copy(ref, ref, send_sem.at[which]).wait()

    loads = [
        pltpu.make_async_copy(a, b, in_sem.at[i])
        for i, (a, b) in enumerate(
            (
                (w_hbm, w_ref), (q_hbm, q_ref), (k_hbm, k_ref), (v_hbm, v_ref), (g_hbm, g_ref),
                (row_hbm, row_tab), (col_hbm, col_tab),
            )
        )
    ]
    for load in loads:
        load.start()

    around = [(d, x) for d in (4, 3, 5, 2, 6, 1, 7, 0) for x in (1, 0)]
    sides = [(((y + d) % 8) * 2 + (xh + x) % 2, 3 * (2 * d + x) + 1) for d, x in around]

    def rounds(one, low, high):
        def step(turn, carry):
            for i in range(16):
                one(((z + turn + sides[i][1]) % 8) * 16 + sides[i][0])
            return carry

        lax.fori_loop(low, min(high, 7), step, 0)
        if high == 8:
            for i in range(16):
                distance = (7 + sides[i][1]) % 8
                if around[i] != (0, 0) or distance != 0:
                    one(((z + distance) % 8) * 16 + sides[i][0])

    barrier = pltpu.get_barrier_semaphore()

    def greet(to_seq, to_rep):
        pl.semaphore_signal(
            barrier, inc=1, device_id={"seq": to_seq, "rep": to_rep}, device_id_type=MESH
        )

    rounds(lambda to: greet(to, rep), 0, 8)
    rep_core, rep_x = xl * 2 + (1 - core), (1 - xl) * 2 + core
    others = [rep_core, rep_x, (1 - xl) * 2 + (1 - core)]
    for to in others:
        greet(seq, to)

    loads[0].wait()
    w_val = w_ref[...].astype(F32)
    for b in range(8):
        w_f32[4 * b : 4 * b + 4, :] = w_val[:, 128 * b : 128 * b + 128]
    w_own[...] = w_f32[pl.ds(pl.multiple_of(8 * rep, 8), 8), :].astype(BF16)
    w_got[pl.ds(seq, 1)] = w_own[...][None]

    def pack(send, *tensors):
        for h in range(2):
            lanes = slice(256 + 128 * h, 384 + 128 * h)
            for c in range(4):
                rows = slice(128 * c, 128 * c + 128)
                parts = [t[rows, lanes].astype(F32).reshape(16, 8, 128) for t in tensors]
                whole = parts[0] if len(parts) == 1 else jnp.concatenate(parts, axis=1)
                send[64 * h + 16 * c : 64 * h + 16 * c + 16] = whole.astype(BF16)

    def keep(send, recv):
        recv[pl.ds(seq, 1)] = send[pl.ds(seq, 1)]

    loads[1].wait()
    loads[2].wait()
    pack(send_qk, q_ref, k_ref)
    keep(send_qk, recv_qk)
    loads[3].wait()
    pack(send_v, v_ref)
    keep(send_v, recv_v)

    def exchange(send, recv, which, low, high):
        def one(to):
            remote(send.at[to], recv.at[seq], which, to, rep).start()

        rounds(one, low, high)

    def share_weights(which):
        def one(to):
            remote(w_own, w_got.at[seq], which, to, rep).start()

        rounds(one, 0, 8)

    pl.semaphore_wait(barrier, SEQ - 1 + 3)

    def spread(recv, count):
        for c in range(8):
            stage[16 * count * c : 16 * count * (c + 1), :] = (
                recv[16 * c : 16 * c + 16].astype(F32).reshape(16 * count, 128)
            )

    def gather(send, count):
        for c in range(8):
            send[16 * c : 16 * c + 16] = (
                stage2[16 * count * c : 16 * count * (c + 1), :]
                .reshape(16, count, 128)
                .astype(BF16)
            )

    def unit(u, count):
        return pl.ds(u, 128, stride=count)

    def whole(ref):
        return ref.at[pl.ds(0, SEQ - 1)]

    strided = z >= 4

    @pl.when(strided)
    def _():
        share_weights(W_STR)

    exchange(send_qk, recv_qk, G_QK, 0, 8)

    loads[5].wait()
    loads[6].wait()
    lane = lax.broadcasted_iota(jnp.int32, (64, 128), 1)
    row = lax.broadcasted_iota(jnp.int32, (64, 128), 0)
    for i in range(8):
        for j in range(i // 2 + 1):
            left = (row_tab[i, 2 * j].astype(F32) - 1.0) * -NEG
            right = (row_tab[i, 2 * j + 1].astype(F32) - 1.0) * -NEG
            bias = jnp.where(lane < 64, left, right)
            if j == i // 2:
                bias = jnp.where(lane + 128 * j <= row + 64 * i, bias, NEG)
            row_bias[64 * i : 64 * i + 64, 128 * j : 128 * j + 128] = bias
    lane = lax.broadcasted_iota(jnp.int32, (16, 128), 1)
    row = lax.broadcasted_iota(jnp.int32, (16, 128), 0)
    for i in range(8):
        bias = jnp.full((16, 128), NEG, F32)
        for j in range(i + 1):
            seen = (col_tab[i, j].astype(F32) - 1.0) * -NEG
            bias = jnp.where(lane // 16 == j, seen, bias)
        col_bias[16 * i : 16 * i + 16, :] = jnp.where(lane <= row + 16 * i, bias, NEG)
    def row_forward(h):
        lanes = slice(128 * h, 128 * h + 128)
        for b in range(4):
            n = 128 * (b + 1)
            rows = slice(128 * b, n)
            s = nt(q_ref[rows, lanes], k_ref[:n, lanes]) * SCALE + row_bias[rows, :n]
            e = jnp.exp(s - jnp.max(s, axis=1, keepdims=True))
            p = e * (1.0 / jnp.sum(e, axis=1, keepdims=True))
            probs[h, rows, :n] = p
            out[rows, lanes] = nn(p.astype(BF16), v_ref[:n, lanes]).astype(BF16)

    def row_backward(h):
        lanes = slice(128 * h, 128 * h + 128)
        for b in (3, 2, 1, 0):
            n = 128 * (b + 1)
            rows = slice(128 * b, n)
            p = probs[h, rows, :n]
            g = grad[rows, lanes]
            dp = nt(g, v_ref[:n, lanes])
            inner = jnp.sum(p * dp, axis=1, keepdims=True)
            ds = (p * (dp - inner) * SCALE).astype(BF16)
            dq_ref[rows, lanes] = nn(ds, k_ref[:n, lanes]).astype(BF16)
            dv = tn(p.astype(BF16), g)
            dk = tn(ds, q_ref[rows, lanes])
            if b == 3:
                dv_acc[...] = dv
                dk_acc[...] = dk
            else:
                dv_acc[:n, :] += dv
                dk_acc[:n, :] += dk
        dv_ref[:, lanes] = dv_acc[...].astype(BF16)
        dk_ref[:, lanes] = dk_acc[...].astype(BF16)

    upper = lax.broadcasted_iota(jnp.int32, (32, 8, 128), 1) < 4

    def arrived_weights(which, mine, half):
        @pl.when(mine)
        def _():
            arrived(w_got.at[pl.ds(0, 63)], which)

        @pl.when(jnp.logical_not(mine))
        def _():
            arrived(w_got.at[pl.ds(0, 64)], which)

        pairs = w_got[64 * half : 64 * half + 64].astype(F32).reshape(32, 2, 8, 128)
        even, odd = pairs[:, 0], pairs[:, 1]
        left = jnp.where(upper, even, pltpu.roll(odd, 4, 1)).reshape(256, 128)
        right = jnp.where(upper, pltpu.roll(even, 4, 1), odd).reshape(256, 128)
        w_x[pl.ds(half, 1), pl.ds(rep, 1)] = (
            jnp.concatenate((left, right), axis=1).astype(BF16)[None, None]
        )

    def share_quarter(which_x, which_core, half):
        mine = w_x.at[half, rep]
        remote(mine, mine, which_x, seq, rep_x).start()
        remote(mine, mine, which_core, seq, rep_core).start()

    def relay_quarter(which_x, which_core, half):
        arrived(w_x.at[half, 0], which_x)
        theirs = w_x.at[half, rep_x]
        remote(theirs, theirs, which_core, seq, rep_core).start()

    def arrived_quarters(which_core, half):
        arrived(w_x.at[half, pl.ds(0, 2)], which_core)

    def quarters(ref):
        return ref.at[pl.ds(0, 3)]

    def attention_gradient(half):
        for c in range(4):
            rows = slice(128 * c, 128 * c + 128)
            total = nt(g_ref[rows, 0:256], w_x[half, 0])
            for r in range(1, 4):
                total += nt(g_ref[rows, 256 * r : 256 * r + 256], w_x[half, r])
            grad[rows, 256 * half : 256 * half + 256] = total.astype(BF16)

    def weight_terms(half, which):
        lanes = slice(256 * half, 256 * half + 256)
        for r in range(4):
            product = tn(out[:, lanes], g_ref[:, 256 * r : 256 * r + 256])
            term[half, r] = product
            term_b[half, r] = product.astype(BF16)
        for i in range(2):
            remote(
                term_b.at[half, 2 * i + 1 - core], term_got.at[half, i], which, seq, rep_core
            ).start()

    def chip_sums(half, which_core, which_x):
        arrived(term_got.at[half], which_core)
        term_own[half] = term[half, rep] + term_got[half, xl].astype(F32)
        term_away[half] = (term[half, rep_x] + term_got[half, 1 - xl].astype(F32)).astype(BF16)
        remote(term_away.at[half], term_near.at[half], which_x, seq, rep_x).start()

    def weight_sums(half, which_x):
        arrived(term_near.at[half], which_x)
        total = term_own[half] + term_near[half].astype(F32)
        left = total[:, 0:128].reshape(32, 8, 128)
        right = total[:, 128:256].reshape(32, 8, 128)
        even = jnp.where(upper, left, pltpu.roll(right, 4, 1))
        odd = jnp.where(upper, pltpu.roll(left, 4, 1), right)
        sum_own[64 * half : 64 * half + 64] = (
            jnp.stack((even, odd), axis=1).reshape(64, 8, 128).astype(BF16)
        )

        def one(to):
            remote(sum_own.at[to], sum_got.at[seq], S_ALL, to, rep).start()

        def step(turn, carry):
            for i in range(16):
                if around[i] != (0, 0):
                    one((4 * half + (z + turn + sides[i][1]) % 4) * 16 + sides[i][0])
            return carry

        lax.fori_loop(0, 4, step, 0)
        here = sides[-1][0]
        for d in (1, 2, 3):
            one((4 * half + (z + d) % 4) * 16 + here)
        mine = z // 4 == half

        @pl.when(jnp.logical_not(mine))
        def _():
            one((4 * half + z % 4) * 16 + here)

        @pl.when(mine)
        def _():
            sum_got[pl.ds(seq, 1)] = sum_own[pl.ds(seq, 1)]

    row_forward(0)
    row_forward(1)
    arrived_weights(W_STR, strided, 1)
    share_quarter(X_STR, C_STR, 1)
    exchange(send_v, recv_v, G_V, 0, 8)

    @pl.when(jnp.logical_not(strided))
    def _():
        share_weights(W_ROW)

    loads[4].wait()
    weight_terms(0, TC_ROW)
    relay_quarter(X_STR, C_STR, 1)
    chip_sums(0, TC_ROW, TX_ROW)
    arrived_quarters(C_STR, 1)
    attention_gradient(1)
    pack(send_g, grad)
    keep(send_g, recv_g)
    exchange(send_g, recv_g, G_G, 0, 8)

    arrived(whole(recv_qk), G_QK)
    spread(recv_qk, 16)
    for u in range(8):
        q = stage[unit(u, 16), :].astype(BF16)
        k = stage[unit(8 + u, 16), :].astype(BF16)
        unit_q[u] = q
        unit_k[u] = k
        s = nt(q, k) * SCALE + col_bias[...]
        e = jnp.exp(s - jnp.max(s, axis=1, keepdims=True))
        unit_p[u] = e * (1.0 / jnp.sum(e, axis=1, keepdims=True))
    arrived(whole(recv_v), G_V)
    spread(recv_v, 8)
    for u in range(8):
        v = stage[unit(u, 8), :].astype(BF16)
        unit_v[u] = v
        stage2[unit(u, 8), :] = nn(unit_p[u].astype(BF16), v)
    gather(back_o, 8)
    keep(back_o, got_o)
    sent(whole(send_qk), G_QK)
    sent(whole(send_v), G_V)
    exchange(back_o, got_o, B_O, 0, 8)

    arrived_weights(W_ROW, jnp.logical_not(strided), 0)
    share_quarter(X_ROW, C_ROW, 0)
    arrived(whole(recv_g), G_G)
    spread(recv_g, 8)
    for u in range(8):
        g = stage[unit(u, 8), :].astype(BF16)
        unit_g[u] = g
        stage2[unit(u, 8), :] = tn(unit_p[u].astype(BF16), g)
    gather(back_v, 8)
    keep(back_v, got_v)
    exchange(back_v, got_v, B_V, 0, 8)
    for u in range(8):
        p = unit_p[u]
        dp = nt(unit_g[u], unit_v[u])
        inner = jnp.sum(p * dp, axis=1, keepdims=True)
        ds = (p * (dp - inner) * SCALE).astype(BF16)
        stage2[unit(u, 16), :] = nn(ds, unit_k[u])
        stage2[unit(8 + u, 16), :] = tn(ds, unit_q[u])
    gather(back_qk, 16)
    keep(back_qk, got_qk)
    exchange(back_qk, got_qk, B_QK, 0, 8)

    def unpack(got, *tensors):
        for h in range(2):
            lanes = slice(256 + 128 * h, 384 + 128 * h)
            for c in range(4):
                rows = slice(128 * c, 128 * c + 128)
                part = got[64 * h + 16 * c : 64 * h + 16 * c + 16].astype(F32)
                for i, t in enumerate(tensors):
                    t[rows, lanes] = part[:, 8 * i : 8 * i + 8, :].reshape(128, 128).astype(BF16)

    relay_quarter(X_ROW, C_ROW, 0)
    weight_sums(0, TX_ROW)
    arrived(whole(got_o), B_O)
    unpack(got_o, out)
    weight_terms(1, TC_STR)
    arrived_quarters(C_ROW, 0)
    attention_gradient(0)
    chip_sums(1, TC_STR, TX_STR)
    row_backward(0)
    row_backward(1)
    weight_sums(1, TX_STR)

    stores = [
        pltpu.make_async_copy(a, b, out_sem.at[i])
        for i, (a, b) in enumerate(
            ((dq_ref, dq_hbm), (dk_ref, dk_hbm), (dv_ref, dv_hbm), (wg_ref, wg_hbm))
        )
    ]
    arrived(whole(got_v), B_V)
    unpack(got_v, dv_ref)
    stores[2].start()
    arrived(whole(got_qk), B_QK)
    unpack(got_qk, dq_ref, dk_ref)
    stores[0].start()
    stores[1].start()

    arrived(whole(sum_got), S_ALL)
    total = sum_got[0:16].astype(F32)
    for i in range(1, 8):
        total += sum_got[16 * i : 16 * i + 16].astype(F32)
    total = jnp.sum(total, axis=0)
    last_own[...] = total * factor
    for to in others:
        remote(last_own, last_got.at[rep], S_REP, seq, to).start()
    last_got[pl.ds(rep, 1)] = last_own[...][None]
    arrived(quarters(last_got), S_REP)
    for r in range(4):
        wg_ref[:, 256 * r : 256 * r + 128] = last_got[r, 0:4, :]
        wg_ref[:, 256 * r + 128 : 256 * r + 256] = last_got[r, 4:8, :]

    stores[3].start()
    for store in stores:
        store.wait()

    @pl.when(strided)
    def _():
        sent(whole(w_got), W_STR)

    @pl.when(jnp.logical_not(strided))
    def _():
        sent(whole(w_got), W_ROW)

    for half, which_x, which_core in ((0, X_ROW, C_ROW), (1, X_STR, C_STR)):
        sent(w_x.at[half, 0], which_x)
        sent(w_x.at[half, pl.ds(0, 2)], which_core)
    for which, ref in ((G_G, send_g), (B_O, back_o), (B_V, back_v), (B_QK, back_qk)):
        sent(whole(ref), which)
    for half, which_core, which_x in ((0, TC_ROW, TX_ROW), (1, TC_STR, TX_STR)):
        sent(term_got.at[half], which_core)
        sent(term_near.at[half], which_x)
    sent(whole(sum_got), S_ALL)
    sent(quarters(last_got), S_REP)


def finish(*refs):
    ins, outs, held, in_sem, out_sem = refs[:4], refs[4:8], refs[8:12], refs[12], refs[13]
    into = [pltpu.make_async_copy(a, b, in_sem.at[i]) for i, (a, b) in enumerate(zip(ins, held))]
    onto = [pltpu.make_async_copy(a, b, out_sem.at[i]) for i, (a, b) in enumerate(zip(held, outs))]
    for copy in into:
        copy.start()
    for first, second in zip(into, onto):
        first.wait()
        second.start()
    for copy in onto:
        copy.wait()


def body(queries, key_vectors, value_vectors, out_grad, out_weight, row_blocks, column_blocks):
    token_count = lax.axis_size("rep") * lax.axis_size("seq") * COLS
    factor = 1.0 / math.sqrt(token_count)
    vmem = pltpu.VMEM
    hbm = pl.BlockSpec(memory_space=pl.ANY)
    grads = jax.ShapeDtypeStruct((COLS, FEAT), BF16)
    one = vmem((SEQ, 8, 128), BF16)
    two = vmem((SEQ, 16, 128), BF16)
    units = vmem((8, 128, 128), BF16)
    scratch = [
        vmem((COLS, FEAT), BF16), vmem((COLS, FEAT), BF16), vmem((COLS, FEAT), BF16),
        vmem((4, MODEL), F32),
        vmem((COLS, FEAT), BF16), vmem((COLS, FEAT), BF16), vmem((COLS, FEAT), BF16),
        vmem((COLS, MODEL), BF16), vmem((4, MODEL), BF16),
        pltpu.SMEM((8, 8), jnp.int32), pltpu.SMEM((8, 8), jnp.int32),
        vmem((32, 128), F32), vmem((8, 128), BF16), one, vmem((2, 4, 256, 256), BF16),
        vmem((COLS, COLS), F32), vmem((SEQ, SEQ), F32),
        vmem((COLS, FEAT), BF16), vmem((COLS, FEAT), BF16), vmem((2, COLS, COLS), F32),
        vmem((COLS, HEAD), F32), vmem((COLS, HEAD), F32),
        two, one, one, two, one, one, one, one, two, one, one, two,
        vmem((SEQ * 16, 128), F32), vmem((SEQ * 16, 128), F32),
        units, units, units, units, vmem((8, 128, 128), F32),
        vmem((2, 4, 256, 256), F32), vmem((2, 4, 256, 256), BF16), vmem((2, 2, 256, 256), BF16),
        vmem((2, 256, 256), F32), vmem((2, 256, 256), BF16), vmem((2, 256, 256), BF16),
        one, one, vmem((8, 128), F32), vmem((4, 8, 128), F32),
        pltpu.SemaphoreType.DMA((7,)),
        pltpu.SemaphoreType.DMA((4,)),
        pltpu.SemaphoreType.DMA((18,)),
        pltpu.SemaphoreType.DMA((18,)),
    ]
    results = (grads, grads, grads, jax.ShapeDtypeStruct((4, MODEL), F32))
    raw = pl.pallas_call(
        functools.partial(kernel, factor),
        out_shape=results,
        in_specs=[hbm] * 7,
        out_specs=(hbm,) * 4,
        scratch_shapes=scratch,
        compiler_params=pltpu.CompilerParams(
            collective_id=0, has_side_effects=True, vmem_limit_bytes=56 * 2**20
        ),
        cost_estimate=pl.CostEstimate(
            flops=2_500_000_000, bytes_accessed=5_000_000, transcendentals=800_000
        ),
    )(
        queries.reshape(COLS, FEAT), key_vectors.reshape(COLS, FEAT),
        value_vectors.reshape(COLS, FEAT), out_grad.reshape(COLS, MODEL),
        out_weight, row_blocks, column_blocks,
    )
    query_grad, key_grad, value_grad, weight_grad = pl.pallas_call(
        finish,
        out_shape=results,
        in_specs=[hbm] * 4,
        out_specs=(hbm,) * 4,
        scratch_shapes=[
            vmem((COLS, FEAT), BF16), vmem((COLS, FEAT), BF16), vmem((COLS, FEAT), BF16),
            vmem((4, MODEL), F32), pltpu.SemaphoreType.DMA((4,)), pltpu.SemaphoreType.DMA((4,)),
        ],
        compiler_params=pltpu.CompilerParams(vmem_limit_bytes=56 * 2**20),
    )(*raw)
    shape = (1, 1, COLS, FEAT)
    return (
        query_grad.reshape(shape), key_grad.reshape(shape), value_grad.reshape(shape), weight_grad
    )


def solution(mesh):
    return jax.shard_map(
        body,
        mesh=mesh,
        in_specs=(
            P("rep", "seq", None, None),
            P("rep", "seq", None, None),
            P("rep", "seq", None, None),
            P("rep", "seq", None, None),
            P("seq", None),
            P(),
            P(),
        ),
        out_specs=(
            P("rep", "seq", None, None),
            P("rep", "seq", None, None),
            P("rep", "seq", None, None),
            P("seq", None),
        ),
        check_vma=False,
    )
```

```python
import functools
import math

import jax
import jax.numpy as jnp
from jax import lax
from jax.experimental import pallas as pl
from jax.experimental.pallas import tpu as pltpu
from jax.sharding import PartitionSpec as P

MESH = pl.DeviceIdType.MESH
F32 = jnp.float32
BF16 = jnp.bfloat16
NEG = -1e30

HEAD = 128
SCALE = 1.0 / math.sqrt(HEAD)
COLS = 512
FEAT = 512
MODEL = 1024
SEQ = 128

(
    W_ROW, W_STR, X_ROW, X_STR, C_ROW, C_STR, G_QK, G_V, G_G, B_O, B_V, B_QK,
    TC_ROW, TC_STR, TX_ROW, TX_STR, S_ALL, S_REP,
) = range(18)


def nn(a, b):
    return lax.dot_general(a, b, (((1,), (0,)), ((), ())), preferred_element_type=F32)


def nt(a, b):
    return lax.dot_general(a, b, (((1,), (1,)), ((), ())), preferred_element_type=F32)


def tn(a, b):
    return lax.dot_general(a, b, (((0,), (0,)), ((), ())), preferred_element_type=F32)


def kernel(
    factor,
    q_hbm, k_hbm, v_hbm, g_hbm, w_hbm, row_hbm, col_hbm,
    dq_hbm, dk_hbm, dv_hbm, wg_hbm,
    dq_ref, dk_ref, dv_ref, wg_ref,
    q_ref, k_ref, v_ref, g_ref, w_ref, row_tab, col_tab,
    w_f32, w_own, w_got, w_x, row_bias, col_bias,
    grad, out, probs, dk_acc, dv_acc,
    send_qk, send_v, send_g, recv_qk, recv_v, recv_g,
    back_o, back_v, back_qk, got_o, got_v, got_qk,
    stage, stage2, unit_q, unit_k, unit_v, unit_g, unit_p,
    term, term_b, term_got, term_own, term_away, term_near, sum_own, sum_got, last_own, last_got,
    in_sem, out_sem, send_sem, recv_sem,
):
    seq = lax.axis_index("seq")
    rep = lax.axis_index("rep")
    z, y, xh = seq // 16, (seq // 2) % 8, seq % 2
    xl, core = rep // 2, rep % 2

    def remote(src, dst, which, to_seq, to_rep):
        return pltpu.make_async_remote_copy(
            src_ref=src, dst_ref=dst, send_sem=send_sem.at[which], recv_sem=recv_sem.at[which],
            device_id={"seq": to_seq, "rep": to_rep}, device_id_type=MESH,
        )

    def arrived(ref, which):
        pltpu.make_async_copy(ref, ref, recv_sem.at[which]).wait()

    def sent(ref, which):
        pltpu.make_async_copy(ref, ref, send_sem.at[which]).wait()

    loads = [
        pltpu.make_async_copy(a, b, in_sem.at[i])
        for i, (a, b) in enumerate(
            (
                (w_hbm, w_ref), (q_hbm, q_ref), (k_hbm, k_ref), (v_hbm, v_ref), (g_hbm, g_ref),
                (row_hbm, row_tab), (col_hbm, col_tab),
            )
        )
    ]
    for load in loads:
        load.start()

    around = [(d, x) for d in (4, 3, 5, 2, 6, 1, 7, 0) for x in (1, 0)]
    sides = [(((y + d) % 8) * 2 + (xh + x) % 2, 3 * (2 * d + x) + 1) for d, x in around]

    def rounds(one, low, high):
        def step(turn, carry):
            for i in range(16):
                one(((z + turn + sides[i][1]) % 8) * 16 + sides[i][0])
            return carry

        lax.fori_loop(low, min(high, 7), step, 0)
        if high == 8:
            for i in range(16):
                distance = (7 + sides[i][1]) % 8
                if around[i] != (0, 0) or distance != 0:
                    one(((z + distance) % 8) * 16 + sides[i][0])

    barrier = pltpu.get_barrier_semaphore()

    def greet(to_seq, to_rep):
        pl.semaphore_signal(
            barrier, inc=1, device_id={"seq": to_seq, "rep": to_rep}, device_id_type=MESH
        )

    rounds(lambda to: greet(to, rep), 0, 8)
    rep_core, rep_x = xl * 2 + (1 - core), (1 - xl) * 2 + core
    others = [rep_core, rep_x, (1 - xl) * 2 + (1 - core)]
    for to in others:
        greet(seq, to)

    loads[0].wait()
    w_val = w_ref[...].astype(F32)
    for b in range(8):
        w_f32[4 * b : 4 * b + 4, :] = w_val[:, 128 * b : 128 * b + 128]
    w_own[...] = w_f32[pl.ds(pl.multiple_of(8 * rep, 8), 8), :].astype(BF16)
    w_got[pl.ds(seq, 1)] = w_own[...][None]

    def pack(send, *tensors):
        for h in range(2):
            lanes = slice(256 + 128 * h, 384 + 128 * h)
            for c in range(4):
                rows = slice(128 * c, 128 * c + 128)
                parts = [t[rows, lanes].astype(F32).reshape(16, 8, 128) for t in tensors]
                whole = parts[0] if len(parts) == 1 else jnp.concatenate(parts, axis=1)
                send[64 * h + 16 * c : 64 * h + 16 * c + 16] = whole.astype(BF16)

    def keep(send, recv):
        recv[pl.ds(seq, 1)] = send[pl.ds(seq, 1)]

    loads[1].wait()
    loads[2].wait()
    pack(send_qk, q_ref, k_ref)
    keep(send_qk, recv_qk)
    loads[3].wait()
    pack(send_v, v_ref)
    keep(send_v, recv_v)

    def exchange(send, recv, which, low, high):
        def one(to):
            remote(send.at[to], recv.at[seq], which, to, rep).start()

        rounds(one, low, high)

    def share_weights(which):
        def one(to):
            remote(w_own, w_got.at[seq], which, to, rep).start()

        rounds(one, 0, 8)

    pl.semaphore_wait(barrier, SEQ - 1 + 3)

    def spread(recv, count):
        for c in range(8):
            stage[16 * count * c : 16 * count * (c + 1), :] = (
                recv[16 * c : 16 * c + 16].astype(F32).reshape(16 * count, 128)
            )

    def gather(send, count):
        for c in range(8):
            send[16 * c : 16 * c + 16] = (
                stage2[16 * count * c : 16 * count * (c + 1), :]
                .reshape(16, count, 128)
                .astype(BF16)
            )

    def unit(u, count):
        return pl.ds(u, 128, stride=count)

    def whole(ref):
        return ref.at[pl.ds(0, SEQ - 1)]

    strided = z >= 4

    @pl.when(strided)
    def _():
        share_weights(W_STR)

    exchange(send_qk, recv_qk, G_QK, 0, 8)
    exchange(send_v, recv_v, G_V, 0, 4)

    loads[5].wait()
    loads[6].wait()
    lane = lax.broadcasted_iota(jnp.int32, (64, 128), 1)
    row = lax.broadcasted_iota(jnp.int32, (64, 128), 0)
    for i in range(8):
        for j in range(i // 2 + 1):
            left = (row_tab[i, 2 * j].astype(F32) - 1.0) * -NEG
            right = (row_tab[i, 2 * j + 1].astype(F32) - 1.0) * -NEG
            bias = jnp.where(lane < 64, left, right)
            if j == i // 2:
                bias = jnp.where(lane + 128 * j <= row + 64 * i, bias, NEG)
            row_bias[64 * i : 64 * i + 64, 128 * j : 128 * j + 128] = bias
    lane = lax.broadcasted_iota(jnp.int32, (16, 128), 1)
    row = lax.broadcasted_iota(jnp.int32, (16, 128), 0)
    for i in range(8):
        bias = jnp.full((16, 128), NEG, F32)
        for j in range(i + 1):
            seen = (col_tab[i, j].astype(F32) - 1.0) * -NEG
            bias = jnp.where(lane // 16 == j, seen, bias)
        col_bias[16 * i : 16 * i + 16, :] = jnp.where(lane <= row + 16 * i, bias, NEG)
    def row_forward(h):
        lanes = slice(128 * h, 128 * h + 128)
        for b in range(4):
            n = 128 * (b + 1)
            rows = slice(128 * b, n)
            s = nt(q_ref[rows, lanes], k_ref[:n, lanes]) * SCALE + row_bias[rows, :n]
            e = jnp.exp(s - jnp.max(s, axis=1, keepdims=True))
            p = e * (1.0 / jnp.sum(e, axis=1, keepdims=True))
            probs[h, rows, :n] = p
            out[rows, lanes] = nn(p.astype(BF16), v_ref[:n, lanes]).astype(BF16)

    def row_backward(h):
        lanes = slice(128 * h, 128 * h + 128)
        for b in (3, 2, 1, 0):
            n = 128 * (b + 1)
            rows = slice(128 * b, n)
            p = probs[h, rows, :n]
            g = grad[rows, lanes]
            dp = nt(g, v_ref[:n, lanes])
            inner = jnp.sum(p * dp, axis=1, keepdims=True)
            ds = (p * (dp - inner) * SCALE).astype(BF16)
            dq_ref[rows, lanes] = nn(ds, k_ref[:n, lanes]).astype(BF16)
            dv = tn(p.astype(BF16), g)
            dk = tn(ds, q_ref[rows, lanes])
            if b == 3:
                dv_acc[...] = dv
                dk_acc[...] = dk
            else:
                dv_acc[:n, :] += dv
                dk_acc[:n, :] += dk
        dv_ref[:, lanes] = dv_acc[...].astype(BF16)
        dk_ref[:, lanes] = dk_acc[...].astype(BF16)

    upper = lax.broadcasted_iota(jnp.int32, (32, 8, 128), 1) < 4

    def arrived_weights(which, mine, half):
        @pl.when(mine)
        def _():
            arrived(w_got.at[pl.ds(0, 63)], which)

        @pl.when(jnp.logical_not(mine))
        def _():
            arrived(w_got.at[pl.ds(0, 64)], which)

        pairs = w_got[64 * half : 64 * half + 64].astype(F32).reshape(32, 2, 8, 128)
        even, odd = pairs[:, 0], pairs[:, 1]
        left = jnp.where(upper, even, pltpu.roll(odd, 4, 1)).reshape(256, 128)
        right = jnp.where(upper, pltpu.roll(even, 4, 1), odd).reshape(256, 128)
        w_x[pl.ds(half, 1), pl.ds(rep, 1)] = (
            jnp.concatenate((left, right), axis=1).astype(BF16)[None, None]
        )

    def share_quarter(which_x, which_core, half):
        mine = w_x.at[half, rep]
        remote(mine, mine, which_x, seq, rep_x).start()
        remote(mine, mine, which_core, seq, rep_core).start()

    def relay_quarter(which_x, which_core, half):
        arrived(w_x.at[half, 0], which_x)
        theirs = w_x.at[half, rep_x]
        remote(theirs, theirs, which_core, seq, rep_core).start()

    def arrived_quarters(which_core, half):
        arrived(w_x.at[half, pl.ds(0, 2)], which_core)

    def quarters(ref):
        return ref.at[pl.ds(0, 3)]

    def attention_gradient(half):
        for c in range(4):
            rows = slice(128 * c, 128 * c + 128)
            total = nt(g_ref[rows, 0:256], w_x[half, 0])
            for r in range(1, 4):
                total += nt(g_ref[rows, 256 * r : 256 * r + 256], w_x[half, r])
            grad[rows, 256 * half : 256 * half + 256] = total.astype(BF16)

    def weight_terms(half, which):
        lanes = slice(256 * half, 256 * half + 256)
        for r in range(4):
            product = tn(out[:, lanes], g_ref[:, 256 * r : 256 * r + 256])
            term[half, r] = product
            term_b[half, r] = product.astype(BF16)
        for i in range(2):
            remote(
                term_b.at[half, 2 * i + 1 - core], term_got.at[half, i], which, seq, rep_core
            ).start()

    def chip_sums(half, which_core, which_x):
        arrived(term_got.at[half], which_core)
        term_own[half] = term[half, rep] + term_got[half, xl].astype(F32)
        term_away[half] = (term[half, rep_x] + term_got[half, 1 - xl].astype(F32)).astype(BF16)
        remote(term_away.at[half], term_near.at[half], which_x, seq, rep_x).start()

    def weight_sums(half, which_x):
        arrived(term_near.at[half], which_x)
        total = term_own[half] + term_near[half].astype(F32)
        left = total[:, 0:128].reshape(32, 8, 128)
        right = total[:, 128:256].reshape(32, 8, 128)
        even = jnp.where(upper, left, pltpu.roll(right, 4, 1))
        odd = jnp.where(upper, pltpu.roll(left, 4, 1), right)
        sum_own[64 * half : 64 * half + 64] = (
            jnp.stack((even, odd), axis=1).reshape(64, 8, 128).astype(BF16)
        )

        def one(to):
            remote(sum_own.at[to], sum_got.at[seq], S_ALL, to, rep).start()

        def step(turn, carry):
            for i in range(16):
                if around[i] != (0, 0):
                    one((4 * half + (z + turn + sides[i][1]) % 4) * 16 + sides[i][0])
            return carry

        lax.fori_loop(0, 4, step, 0)
        here = sides[-1][0]
        for d in (1, 2, 3):
            one((4 * half + (z + d) % 4) * 16 + here)
        mine = z // 4 == half

        @pl.when(jnp.logical_not(mine))
        def _():
            one((4 * half + z % 4) * 16 + here)

        @pl.when(mine)
        def _():
            sum_got[pl.ds(seq, 1)] = sum_own[pl.ds(seq, 1)]

    row_forward(0)
    row_forward(1)
    arrived_weights(W_STR, strided, 1)
    share_quarter(X_STR, C_STR, 1)
    exchange(send_v, recv_v, G_V, 4, 8)

    @pl.when(jnp.logical_not(strided))
    def _():
        share_weights(W_ROW)

    loads[4].wait()
    weight_terms(0, TC_ROW)
    relay_quarter(X_STR, C_STR, 1)
    chip_sums(0, TC_ROW, TX_ROW)
    arrived_quarters(C_STR, 1)
    attention_gradient(1)
    pack(send_g, grad)
    keep(send_g, recv_g)
    exchange(send_g, recv_g, G_G, 0, 8)

    arrived(whole(recv_qk), G_QK)
    spread(recv_qk, 16)
    for u in range(8):
        q = stage[unit(u, 16), :].astype(BF16)
        k = stage[unit(8 + u, 16), :].astype(BF16)
        unit_q[u] = q
        unit_k[u] = k
        s = nt(q, k) * SCALE + col_bias[...]
        e = jnp.exp(s - jnp.max(s, axis=1, keepdims=True))
        unit_p[u] = e * (1.0 / jnp.sum(e, axis=1, keepdims=True))
    arrived(whole(recv_v), G_V)
    spread(recv_v, 8)
    for u in range(8):
        v = stage[unit(u, 8), :].astype(BF16)
        unit_v[u] = v
        stage2[unit(u, 8), :] = nn(unit_p[u].astype(BF16), v)
    gather(back_o, 8)
    keep(back_o, got_o)
    sent(whole(send_qk), G_QK)
    sent(whole(send_v), G_V)
    exchange(back_o, got_o, B_O, 0, 8)

    arrived_weights(W_ROW, jnp.logical_not(strided), 0)
    share_quarter(X_ROW, C_ROW, 0)
    arrived(whole(recv_g), G_G)
    spread(recv_g, 8)
    for u in range(8):
        g = stage[unit(u, 8), :].astype(BF16)
        unit_g[u] = g
        stage2[unit(u, 8), :] = tn(unit_p[u].astype(BF16), g)
    gather(back_v, 8)
    keep(back_v, got_v)
    exchange(back_v, got_v, B_V, 0, 8)
    for u in range(8):
        p = unit_p[u]
        dp = nt(unit_g[u], unit_v[u])
        inner = jnp.sum(p * dp, axis=1, keepdims=True)
        ds = (p * (dp - inner) * SCALE).astype(BF16)
        stage2[unit(u, 16), :] = nn(ds, unit_k[u])
        stage2[unit(8 + u, 16), :] = tn(ds, unit_q[u])
    gather(back_qk, 16)
    keep(back_qk, got_qk)
    exchange(back_qk, got_qk, B_QK, 0, 8)

    def unpack(got, *tensors):
        for h in range(2):
            lanes = slice(256 + 128 * h, 384 + 128 * h)
            for c in range(4):
                rows = slice(128 * c, 128 * c + 128)
                part = got[64 * h + 16 * c : 64 * h + 16 * c + 16].astype(F32)
                for i, t in enumerate(tensors):
                    t[rows, lanes] = part[:, 8 * i : 8 * i + 8, :].reshape(128, 128).astype(BF16)

    relay_quarter(X_ROW, C_ROW, 0)
    weight_sums(0, TX_ROW)
    arrived(whole(got_o), B_O)
    unpack(got_o, out)
    weight_terms(1, TC_STR)
    arrived_quarters(C_ROW, 0)
    attention_gradient(0)
    chip_sums(1, TC_STR, TX_STR)
    row_backward(0)
    row_backward(1)
    weight_sums(1, TX_STR)

    stores = [
        pltpu.make_async_copy(a, b, out_sem.at[i])
        for i, (a, b) in enumerate(
            ((dq_ref, dq_hbm), (dk_ref, dk_hbm), (dv_ref, dv_hbm), (wg_ref, wg_hbm))
        )
    ]
    arrived(whole(got_v), B_V)
    unpack(got_v, dv_ref)
    stores[2].start()
    arrived(whole(got_qk), B_QK)
    unpack(got_qk, dq_ref, dk_ref)
    stores[0].start()
    stores[1].start()

    arrived(whole(sum_got), S_ALL)
    total = sum_got[0:16].astype(F32)
    for i in range(1, 8):
        total += sum_got[16 * i : 16 * i + 16].astype(F32)
    total = jnp.sum(total, axis=0)
    last_own[...] = total * factor
    for to in others:
        remote(last_own, last_got.at[rep], S_REP, seq, to).start()
    last_got[pl.ds(rep, 1)] = last_own[...][None]
    arrived(quarters(last_got), S_REP)
    for r in range(4):
        wg_ref[:, 256 * r : 256 * r + 128] = last_got[r, 0:4, :]
        wg_ref[:, 256 * r + 128 : 256 * r + 256] = last_got[r, 4:8, :]

    stores[3].start()
    for store in stores:
        store.wait()

    @pl.when(strided)
    def _():
        sent(whole(w_got), W_STR)

    @pl.when(jnp.logical_not(strided))
    def _():
        sent(whole(w_got), W_ROW)

    for half, which_x, which_core in ((0, X_ROW, C_ROW), (1, X_STR, C_STR)):
        sent(w_x.at[half, 0], which_x)
        sent(w_x.at[half, pl.ds(0, 2)], which_core)
    for which, ref in ((G_G, send_g), (B_O, back_o), (B_V, back_v), (B_QK, back_qk)):
        sent(whole(ref), which)
    for half, which_core, which_x in ((0, TC_ROW, TX_ROW), (1, TC_STR, TX_STR)):
        sent(term_got.at[half], which_core)
        sent(term_near.at[half], which_x)
    sent(whole(sum_got), S_ALL)
    sent(quarters(last_got), S_REP)


def finish(*refs):
    ins, outs, held, in_sem, out_sem = refs[:4], refs[4:8], refs[8:12], refs[12], refs[13]
    into = [pltpu.make_async_copy(a, b, in_sem.at[i]) for i, (a, b) in enumerate(zip(ins, held))]
    onto = [pltpu.make_async_copy(a, b, out_sem.at[i]) for i, (a, b) in enumerate(zip(held, outs))]
    for copy in into:
        copy.start()
    for first, second in zip(into, onto):
        first.wait()
        second.start()
    for copy in onto:
        copy.wait()


def body(queries, key_vectors, value_vectors, out_grad, out_weight, row_blocks, column_blocks):
    token_count = lax.axis_size("rep") * lax.axis_size("seq") * COLS
    factor = 1.0 / math.sqrt(token_count)
    vmem = pltpu.VMEM
    hbm = pl.BlockSpec(memory_space=pl.ANY)
    grads = jax.ShapeDtypeStruct((COLS, FEAT), BF16)
    one = vmem((SEQ, 8, 128), BF16)
    two = vmem((SEQ, 16, 128), BF16)
    units = vmem((8, 128, 128), BF16)
    scratch = [
        vmem((COLS, FEAT), BF16), vmem((COLS, FEAT), BF16), vmem((COLS, FEAT), BF16),
        vmem((4, MODEL), F32),
        vmem((COLS, FEAT), BF16), vmem((COLS, FEAT), BF16), vmem((COLS, FEAT), BF16),
        vmem((COLS, MODEL), BF16), vmem((4, MODEL), BF16),
        pltpu.SMEM((8, 8), jnp.int32), pltpu.SMEM((8, 8), jnp.int32),
        vmem((32, 128), F32), vmem((8, 128), BF16), one, vmem((2, 4, 256, 256), BF16),
        vmem((COLS, COLS), F32), vmem((SEQ, SEQ), F32),
        vmem((COLS, FEAT), BF16), vmem((COLS, FEAT), BF16), vmem((2, COLS, COLS), F32),
        vmem((COLS, HEAD), F32), vmem((COLS, HEAD), F32),
        two, one, one, two, one, one, one, one, two, one, one, two,
        vmem((SEQ * 16, 128), F32), vmem((SEQ * 16, 128), F32),
        units, units, units, units, vmem((8, 128, 128), F32),
        vmem((2, 4, 256, 256), F32), vmem((2, 4, 256, 256), BF16), vmem((2, 2, 256, 256), BF16),
        vmem((2, 256, 256), F32), vmem((2, 256, 256), BF16), vmem((2, 256, 256), BF16),
        one, one, vmem((8, 128), F32), vmem((4, 8, 128), F32),
        pltpu.SemaphoreType.DMA((7,)),
        pltpu.SemaphoreType.DMA((4,)),
        pltpu.SemaphoreType.DMA((18,)),
        pltpu.SemaphoreType.DMA((18,)),
    ]
    results = (grads, grads, grads, jax.ShapeDtypeStruct((4, MODEL), F32))
    raw = pl.pallas_call(
        functools.partial(kernel, factor),
        out_shape=results,
        in_specs=[hbm] * 7,
        out_specs=(hbm,) * 4,
        scratch_shapes=scratch,
        compiler_params=pltpu.CompilerParams(
            collective_id=0, has_side_effects=True, vmem_limit_bytes=56 * 2**20
        ),
        cost_estimate=pl.CostEstimate(
            flops=2_500_000_000, bytes_accessed=5_000_000, transcendentals=800_000
        ),
    )(
        queries.reshape(COLS, FEAT), key_vectors.reshape(COLS, FEAT),
        value_vectors.reshape(COLS, FEAT), out_grad.reshape(COLS, MODEL),
        out_weight, row_blocks, column_blocks,
    )
    query_grad, key_grad, value_grad, weight_grad = pl.pallas_call(
        finish,
        out_shape=results,
        in_specs=[hbm] * 4,
        out_specs=(hbm,) * 4,
        scratch_shapes=[
            vmem((COLS, FEAT), BF16), vmem((COLS, FEAT), BF16), vmem((COLS, FEAT), BF16),
            vmem((4, MODEL), F32), pltpu.SemaphoreType.DMA((4,)), pltpu.SemaphoreType.DMA((4,)),
        ],
        compiler_params=pltpu.CompilerParams(vmem_limit_bytes=56 * 2**20),
    )(*raw)
    shape = (1, 1, COLS, FEAT)
    return (
        query_grad.reshape(shape), key_grad.reshape(shape), value_grad.reshape(shape), weight_grad
    )


def solution(mesh):
    return jax.shard_map(
        body,
        mesh=mesh,
        in_specs=(
            P("rep", "seq", None, None),
            P("rep", "seq", None, None),
            P("rep", "seq", None, None),
            P("rep", "seq", None, None),
            P("seq", None),
            P(),
            P(),
        ),
        out_specs=(
            P("rep", "seq", None, None),
            P("rep", "seq", None, None),
            P("rep", "seq", None, None),
            P("seq", None),
        ),
        check_vma=False,
    )
```
